256 devices in a mesh: mp: 32 (over z, x), dp: 8 (over y, core).
Axes of the slice: x: 4, y: 4, z: 8, core: 2. Of those that a mesh axis runs over, the one named last changes fastest.
Arguments:
- inputs: bfloat16 [1536, 8192], P('dp', 'mp'), may hold values from -42 to 42
- out_grads: bfloat16 [1536, 16384], P('dp', 'mp'), may hold values from -42 to 42
- weight: bfloat16 [8192, 16384], P('dp', 'mp'), may hold values from -0.25 to 0.25
- enc_in: bfloat16 [8192, 1920], P('mp'), may hold values from -0.0625 to 0.0625
- dec_in: bfloat16 [1920, 8192], P(None, 'mp'), may hold values from -0.125 to 0.125
- enc_out: bfloat16 [16384, 1920], P('mp'), may hold values from -0.046875 to 0.046875
- dec_out: bfloat16 [1920, 16384], P(None, 'mp'), may hold values from -0.125 to 0.125
Outputs:
- post_out: bfloat16 [1536, 16384], P('dp', 'mp')
- grad_in: bfloat16 [1536, 8192], P('dp', 'mp')
The draws below stay inside these ranges and needn't reach their ends.
All inputs are finite; a program needn't handle non-finite values.
Results may differ from the reference program's by a relative error of at most 0.024.
Values may be sent and summed in bfloat16 or wider, within the bound.
A program may use at most 64 MiB of HBM per device.

```python
import jax
import jax.numpy as jnp
from jax import lax

D = 8192
FW = 16384
R = 1920
TOKENS = 1536
N_MP = 32


def ramped(key, rows, cols):
    key_vals = jax.random.fold_in(key, 11)
    column_ramp = 1.0 + 2.0 * jnp.arange(cols, dtype=jnp.float32)[None, :] / cols
    values = jax.random.truncated_normal(key_vals, -4.0, 4.0, (rows, cols), jnp.float32)
    result = values * column_ramp
    return result


def draw_inputs(key, part):
    return ramped(jax.random.fold_in(key, 1), TOKENS, D).astype(jnp.bfloat16)


def draw_out_grads(key, part):
    return ramped(jax.random.fold_in(key, 2), TOKENS, FW).astype(jnp.bfloat16)


def block_levels(own_key, dims, shards, least, high):
    factor_of, own = 1.0, jax.random.fold_in(own_key, 6)
    for dim, blocks in shards:
        heights = jnp.exp(jax.random.uniform(jax.random.fold_in(own, dim), (blocks,), jnp.float32, least / len(shards), high / len(shards)))
        factor_of = factor_of * jnp.repeat(heights, dims[dim] // blocks).reshape([-1 if axis == dim else 1 for axis in range(len(dims))])
    return factor_of


def noise(stream_key, extent, spread, limit, split=(), kind=jnp.bfloat16):
    values = spread * jax.random.normal(stream_key, extent, jnp.float32)
    if split:
        values = values * block_levels(stream_key, extent, split, -0.22, 0.18)
    return jnp.clip(values, -limit, limit).astype(kind)


def setup_inputs(seed: int = 0) -> dict:
    arg_keys = jax.random.split(jax.random.key(seed), 8)
    inputs = draw_inputs(jax.random.fold_in(arg_keys[7], 71), 0)
    out_grads = draw_out_grads(jax.random.fold_in(arg_keys[7], 71), 0)
    weight = noise(arg_keys[2], (D, FW), (D // 16) ** -0.5, 0.25, ((0, 8), (1, 32)))
    enc_in = noise(arg_keys[3], (D, R), D ** -0.5, 0.0625, ((0, 32),))
    dec_in = noise(arg_keys[4], (R, D), R ** -0.5, 0.125, ((1, 32),))
    enc_out = noise(arg_keys[5], (FW, R), FW ** -0.5, 0.046875, ((0, 32),))
    dec_out = noise(arg_keys[6], (R, FW), R ** -0.5, 0.125, ((1, 32),))
    return dict(inputs=inputs, out_grads=out_grads, weight=weight, enc_in=enc_in, dec_in=dec_in, enc_out=enc_out, dec_out=dec_out)


epsilon = 1e-06
step_size = 0.25

def silu_slope(value):
    sig = jax.nn.sigmoid(value)
    return sig * (1.0 + value * (1.0 - sig))

def reference(inputs, out_grads, weight, enc_in, dec_in, enc_out, dec_out):
    factor = step_size / D
    input_wide = inputs.astype(jnp.float32)
    grad_wide = out_grads.astype(jnp.float32)
    input_scale = lax.rsqrt(lax.optimization_barrier(jnp.sum(input_wide * input_wide, axis=1, keepdims=True)) / D + epsilon)
    grad_scale = lax.rsqrt(lax.optimization_barrier(jnp.sum(grad_wide * grad_wide, axis=1, keepdims=True)) / FW + epsilon)
    input_hidden = jax.nn.relu(jnp.dot(inputs, enc_in, preferred_element_type=jnp.float32) * input_scale).astype(jnp.bfloat16)
    grad_hidden = jax.nn.relu(jnp.dot(out_grads, enc_out, preferred_element_type=jnp.float32) * grad_scale).astype(jnp.bfloat16)
    edited_in = (input_wide + jnp.dot(input_hidden, dec_in, preferred_element_type=jnp.float32)).astype(jnp.bfloat16)
    edited_grad = (grad_wide + jnp.dot(grad_hidden, dec_out, preferred_element_type=jnp.float32)).astype(jnp.bfloat16)
    kernel = (jnp.dot(inputs, edited_in.T, preferred_element_type=jnp.float32) * factor).astype(jnp.bfloat16)
    post_full = jnp.dot(inputs, weight, preferred_element_type=jnp.float32) - jnp.dot(kernel, edited_grad, preferred_element_type=jnp.float32)
    post_out = post_full.astype(jnp.bfloat16)
    cotangent = (grad_wide * silu_slope(post_full)).astype(jnp.bfloat16)
    width = FW // N_MP
    weight_blocks = weight.reshape(D, N_MP, width).transpose(1, 0, 2)
    cot_blocks = cotangent.reshape(TOKENS, N_MP, width).transpose(1, 0, 2)

    def add_block(total, pair):
        cot_piece, weight_piece = pair
        part = jnp.dot(cot_piece, weight_piece.T, preferred_element_type=jnp.float32).astype(jnp.bfloat16)
        part = lax.optimization_barrier(part)
        return (total + part.astype(jnp.float32), None)
    back, _ = lax.scan(add_block, jnp.zeros((TOKENS, D), jnp.float32), (cot_blocks, weight_blocks))
    back_kernel = (jnp.dot(cotangent, edited_grad.T, preferred_element_type=jnp.float32) * factor).astype(jnp.bfloat16)
    grad_in = (back - jnp.dot(back_kernel, edited_in, preferred_element_type=jnp.float32)).astype(jnp.bfloat16)
    return (post_out, grad_in)
```

```python
import functools

import jax
import jax.numpy as jnp
from jax import lax
from jax.experimental import pallas as pl
from jax.experimental.pallas import tpu as pltpu
from jax.sharding import PartitionSpec as P

D = 8192
FW = 16384
R = 1920
NZ, NX, NY = 8, 4, 4
TOK = 192
ROWS = TOK // NX
epsilon = 1e-06
FACTOR = 0.25 / D
F32 = jnp.float32
BF16 = jnp.bfloat16
MESH = pl.DeviceIdType.MESH


def nn(a, b):
    return lax.dot_general(a, b, (((1,), (0,)), ((), ())), preferred_element_type=F32)


def nt(a, b):
    return lax.dot_general(a, b, (((1,), (1,)), ((), ())), preferred_element_type=F32)


class Links:
    def __init__(self, send, recv):
        self.send, self.recv, self.used, self.sent = send, recv, 0, []
        mp, dp = lax.axis_index("mp"), lax.axis_index("dp")
        self.z, self.x = mp // NX, mp % NX
        self.y, self.c = dp // 2, dp % 2

    def at(self, z=None, x=None, y=None, c=None):
        z = self.z if z is None else z
        x = self.x if x is None else x
        y = self.y if y is None else y
        c = self.c if c is None else c
        return (z * NX + x, y * 2 + c)

    def copy(self, src, dst, device):
        k = self.used
        self.used += 1
        made = pltpu.make_async_remote_copy(
            src_ref=src, dst_ref=dst, send_sem=self.send.at[k], recv_sem=self.recv.at[k],
            device_id=device, device_id_type=MESH)
        made.start()
        self.sent.append(made)
        return made


class AllReduce:
    def __init__(self, net, part, got_x, row, got_z, full):
        self.net, self.part, self.got_x, self.row, self.got_z, self.full = net, part, got_x, row, got_z, full

    def scatter_x(self):
        n = self.net
        self.a = [n.copy(self.part.at[(n.x + o) % NX], self.got_x.at[o - 1], n.at(x=(n.x + o) % NX))
                  for o in range(1, NX)]

    def scatter_z(self):
        n = self.net
        for made in self.a:
            made.wait_recv()

        def add(k, _):
            total = self.part[n.x, k].astype(F32)
            for o in range(NX - 1):
                total = total + self.got_x[o, k].astype(F32)
            self.row[k] = total.astype(BF16)
            return 0
        lax.fori_loop(0, NZ, add, 0)
        self.b = [n.copy(self.row.at[(n.z + o) % NZ], self.got_z.at[o - 1], n.at(z=(n.z + o) % NZ))
                  for o in range(1, NZ)]

    def gather_z(self):
        n = self.net
        for made in self.b:
            made.wait_recv()
        total = self.row[n.z].astype(F32)
        for o in range(NZ - 1):
            total = total + self.got_z[o].astype(F32)
        self.full[n.x, n.z] = total.astype(BF16)
        self.d = [n.copy(self.full.at[n.x, n.z], self.full.at[n.x, n.z], n.at(z=(n.z + o) % NZ))
                  for o in range(1, NZ)]

    def gather_x(self):
        n = self.net
        for made in self.d:
            made.wait_recv()
        self.e = [n.copy(self.full.at[n.x], self.full.at[n.x], n.at(x=(n.x + o) % NX))
                  for o in range(1, NX)]

    def done(self):
        for made in self.e:
            made.wait_recv()


class GatherDp:
    def __init__(self, net, part):
        self.net, self.part = net, part

    def start(self, src=None):
        n = self.net
        d = n.y * 2 + n.c
        own = self.part(d, None)
        src = own if src is None else src
        self.up = n.copy(src, own, n.at(y=(n.y + 1) % NY))
        self.down = n.copy(src, own, n.at(y=(n.y + NY - 1) % NY))
        self.over = [n.copy(src, own, n.at(c=1 - n.c))]

    def relay(self):
        n = self.net
        below = ((n.y + NY - 1) % NY) * 2 + n.c
        above = ((n.y + 1) % NY) * 2 + n.c
        self.up.wait_recv()
        self.up2 = n.copy(self.part(below, 0), self.part(below, 0), n.at(y=(n.y + 1) % NY))
        self.over.append(n.copy(self.part(below, None), self.part(below, None), n.at(c=1 - n.c)))
        self.down.wait_recv()
        self.down2 = n.copy(self.part(above, 1), self.part(above, 1), n.at(y=(n.y + NY - 1) % NY))
        self.over.append(n.copy(self.part(above, None), self.part(above, None), n.at(c=1 - n.c)))

    def relay_far(self):
        n = self.net
        far = ((n.y + 2) % NY) * 2 + n.c
        self.up2.wait_recv()
        self.over.append(n.copy(self.part(far, 0), self.part(far, 0), n.at(c=1 - n.c)))
        self.down2.wait_recv()
        self.over.append(n.copy(self.part(far, 1), self.part(far, 1), n.at(c=1 - n.c)))

    def done(self):
        for made in self.over:
            made.wait_recv()


class GatherMp:
    def __init__(self, net, block):
        self.net, self.block = net, block

    def start(self):
        n = self.net
        own = self.block.at[n.z, n.x]
        self.a = [n.copy(own, own, n.at(x=(n.x + o) % NX)) for o in range(1, NX)]
        self.s = 0

    def step(self):
        n, s = self.net, self.s
        if s == 0:
            for made in self.a:
                made.wait_recv()
        else:
            self.up.wait_recv()
            if s <= NZ // 2 - 1:
                self.down.wait_recv()
        if s < NZ // 2:
            up = self.block.at[(n.z + NZ - s) % NZ]
            self.up = n.copy(up, up, n.at(z=(n.z + 1) % NZ))
        if s < NZ // 2 - 1:
            down = self.block.at[(n.z + s) % NZ]
            self.down = n.copy(down, down, n.at(z=(n.z + NZ - 1) % NZ))
        self.s += 1


def body(x_hbm, g_hbm, w_hbm, ei_hbm, di_hbm, eo_hbm, do_hbm, post_ref, gin_ref,
         xin, g, w, ei, di, eo, do, part, got_x, row, got_z, full, edits, grads, total, cot,
         bpart, bgot_x, brow, bgot_z, send, recv, load):
    net = Links(send, recv)
    z, x, y, c = net.z, net.x, net.y, net.c
    d = y * 2 + c

    loads = []
    for k, (src, dst) in enumerate(((x_hbm, xin.at[z, x]), (ei_hbm, ei), (g_hbm, g), (eo_hbm, eo),
                                    (di_hbm, di), (do_hbm, do), (w_hbm, w.at[d]))):
        made = pltpu.make_async_copy(src, dst, load.at[k])
        made.start()
        loads.append(made)

    barrier = pltpu.get_barrier_semaphore()
    peers = ([net.at(x=(x + o) % NX) for o in range(1, NX)] + [net.at(z=(z + o) % NZ) for o in range(1, NZ)]
             + [net.at(y=(y + 1) % NY), net.at(y=(y + NY - 1) % NY), net.at(c=1 - c)])
    for peer in peers:
        pl.semaphore_signal(barrier, inc=1, device_id=peer, device_id_type=MESH)
    pl.semaphore_wait(barrier, len(peers))

    def w_part(slot, half):
        return w.at[slot] if half is None else w.at[slot, pl.ds(2 * half, 2)]

    def rows_of(ref):
        def pick(slot, half):
            return ref.at[slot, pl.ds(0, TOK)] if half is None else ref.at[slot, pl.ds(half * (TOK // 2), TOK // 2)]
        return pick

    whole_w = GatherDp(net, w_part)
    whole_w.start(w_hbm)
    loads[0].wait()
    whole_in = GatherMp(net, xin)
    whole_in.start()

    own = xin[z, x]

    def project(value, enc, out):
        for k in range(7):
            block = nn(value, enc[:, 256 * k:256 * k + 256])
            out[:, k] = block.astype(BF16).reshape(NX, ROWS, 256)
        last = nn(value, enc[:, 1792:1920])
        out[:, 7, :, 0:128] = last.astype(BF16).reshape(NX, ROWS, 128)
        wide = value.astype(F32)
        square = wide * wide
        fold = square[:, 0:128]
        for k in range(1, value.shape[1] // 128):
            fold = fold + square[:, 128 * k:128 * k + 128]
        out[:, 7, :, 128:256] = fold.astype(BF16).reshape(NX, ROWS, 128)

    reduce_in, reduce_out, reduce_kernel, reduce_back = [
        AllReduce(net, part.at[k], got_x.at[k], row.at[k], got_z.at[k], full.at[k]) for k in range(4)]

    loads[1].wait()
    project(own, ei, part.at[0])
    reduce_in.scatter_x()
    loads[2].wait()
    loads[3].wait()
    project(g[...], eo, part.at[1])
    reduce_out.scatter_x()
    edits[:, pl.ds(TOK, 256 - TOK)] = jnp.zeros((8, 256 - TOK, 256), BF16)
    grads[:, pl.ds(TOK, 256 - TOK)] = jnp.zeros((8, 256 - TOK, 512), BF16)
    for made in loads[4:]:
        made.wait()
    whole_in.step()
    reduce_in.scatter_z()
    reduce_out.scatter_z()
    reduce_in.gather_z()
    reduce_out.gather_z()
    whole_in.step()
    reduce_in.gather_x()
    reduce_out.gather_x()
    whole_w.relay()

    def edit(value, hidden, dec, features):
        squares = hidden[:, 7, :, 128:256].astype(F32).reshape(TOK, 128)
        scale = lax.rsqrt(jnp.sum(squares, axis=1, keepdims=True) / features + epsilon)
        out = value.astype(F32)
        for k in range(8):
            width = 256 if k < 7 else 128
            h = hidden[:, k, :, 0:width].astype(F32).reshape(TOK, width)
            h = jnp.maximum(h * scale, 0.0).astype(BF16)
            out = out + nn(h, dec[256 * k:256 * k + width, :])
        return out.astype(BF16)

    gather_edits = GatherDp(net, rows_of(edits))
    gather_grads = GatherDp(net, rows_of(grads))
    reduce_in.done()
    edits[d, pl.ds(0, TOK)] = edit(own, full.at[0], di, D)
    gather_edits.start()
    reduce_out.done()
    grads[d, pl.ds(0, TOK)] = edit(g[...], full.at[1], do, FW)
    gather_grads.start()
    gather_edits.relay()
    gather_edits.relay_far()
    gather_edits.done()

    def inner(k, _):
        part[2, :, k] = nt(own, edits[k]).astype(BF16).reshape(NX, ROWS, 256)
        return 0
    lax.fori_loop(0, 8, inner, 0)
    reduce_kernel.scatter_x()
    gather_grads.relay()
    whole_in.step()
    whole_w.relay_far()
    reduce_kernel.scatter_z()
    gather_grads.relay_far()
    whole_in.step()
    reduce_kernel.gather_z()
    whole_w.done()
    whole_in.step()

    total[...] = jnp.zeros_like(total)

    def base(k, _):
        value = nn(xin[k, 0], w[k, 0])
        for j in range(1, NX):
            value = value + nn(xin[k, j], w[k, j])
        total[...] += value
        return 0
    lax.fori_loop(0, NZ, base, 0)
    reduce_kernel.gather_x()
    gather_grads.done()
    reduce_kernel.done()

    def correct(k, _):
        block = (full[2, :, k].astype(F32) * FACTOR).astype(BF16).reshape(TOK, 256)
        total[...] -= nn(block, grads[k])
        return 0
    lax.fori_loop(0, 8, correct, 0)

    def activate(k, _):
        rows = pl.ds(k * ROWS, ROWS)
        post = total[rows, :]
        post_ref[rows, :] = post.astype(BF16)
        sig = jax.nn.sigmoid(post)
        cot[rows, :] = (g[rows, :].astype(F32) * (sig * (1.0 + post * (1.0 - sig)))).astype(BF16)
        return 0
    lax.fori_loop(0, NX, activate, 0)

    def back_inner(k, _):
        part[3, :, k] = nt(cot[...], grads[k]).astype(BF16).reshape(NX, ROWS, 256)
        return 0
    lax.fori_loop(0, 8, back_inner, 0)
    reduce_back.scatter_x()

    def back_for(j):
        def one(k, _):
            bpart[j, k] = nt(cot[...], w[k, j]).astype(BF16)
            return 0
        lax.fori_loop(0, NZ, one, 0)

    first = []
    for o in range(1, NX):
        j = (x + o) % NX
        back_for(j)
        first.append(net.copy(bpart.at[j], bgot_x.at[o - 1], net.at(x=j)))
    back_for(x)
    reduce_back.scatter_z()
    reduce_back.gather_z()
    reduce_back.gather_x()
    for made in first:
        made.wait_recv()

    def back_add(k, _):
        value = bpart[x, k].astype(F32)
        for o in range(NX - 1):
            value = value + bgot_x[o, k].astype(F32)
        brow[k] = value.astype(BF16)
        return 0
    lax.fori_loop(0, NZ, back_add, 0)
    second = [net.copy(brow.at[(z + o) % NZ], bgot_z.at[o - 1], net.at(z=(z + o) % NZ)) for o in range(1, NZ)]
    reduce_back.done()
    result = jnp.zeros((TOK, 256), F32)
    for k in range(8):
        block = (full[3, :, k].astype(F32) * FACTOR).astype(BF16).reshape(TOK, 256)
        result = result - nn(block, edits[k])
    result = result + brow[z].astype(F32)
    for o, made in enumerate(second):
        made.wait_recv()
        result = result + bgot_z[o].astype(F32)
    gin_ref[...] = result.astype(BF16)

    for made in net.sent:
        made.wait_send()


COPIES = 160


def shards(inputs, out_grads, weight, enc_in, dec_in, enc_out, dec_out):
    anywhere = pl.BlockSpec(memory_space=pl.ANY)
    vmem = pl.BlockSpec(memory_space=pltpu.VMEM)
    scratch = [
        pltpu.VMEM((NZ, NX, TOK, 256), BF16),
        pltpu.VMEM((TOK, 512), BF16),
        pltpu.VMEM((8, 4, 256, 512), BF16),
        pltpu.VMEM((256, R), BF16),
        pltpu.VMEM((R, 256), BF16),
        pltpu.VMEM((512, R), BF16),
        pltpu.VMEM((R, 512), BF16),
        pltpu.VMEM((4, NX, NZ, ROWS, 256), BF16),
        pltpu.VMEM((4, NX - 1, NZ, ROWS, 256), BF16),
        pltpu.VMEM((4, NZ, ROWS, 256), BF16),
        pltpu.VMEM((4, NZ - 1, ROWS, 256), BF16),
        pltpu.VMEM((4, NX, NZ, ROWS, 256), BF16),
        pltpu.VMEM((8, 256, 256), BF16),
        pltpu.VMEM((8, 256, 512), BF16),
        pltpu.VMEM((TOK, 512), F32),
        pltpu.VMEM((TOK, 512), BF16),
        pltpu.VMEM((NX, NZ, TOK, 256), BF16),
        pltpu.VMEM((NX - 1, NZ, TOK, 256), BF16),
        pltpu.VMEM((NZ, TOK, 256), BF16),
        pltpu.VMEM((NZ - 1, TOK, 256), BF16),
        pltpu.SemaphoreType.DMA((COPIES,)),
        pltpu.SemaphoreType.DMA((COPIES,)),
        pltpu.SemaphoreType.DMA((7,)),
    ]
    return pl.pallas_call(
        body,
        out_shape=(jax.ShapeDtypeStruct((TOK, 512), BF16), jax.ShapeDtypeStruct((TOK, 256), BF16)),
        in_specs=[anywhere] * 7,
        out_specs=(vmem, vmem),
        scratch_shapes=scratch,
        compiler_params=pltpu.CompilerParams(
            collective_id=0, has_side_effects=True, vmem_limit_bytes=60 * 1024 * 1024),
    )(inputs, out_grads, weight.reshape(4, 256, 512), enc_in, dec_in, enc_out, dec_out)


def solution(mesh):
    in_specs = (
        P("dp", "mp"),
        P("dp", "mp"),
        P("dp", "mp"),
        P("mp", None),
        P(None, "mp"),
        P("mp", None),
        P(None, "mp"),
    )
    out_specs = (P("dp", "mp"), P("dp", "mp"))
    return jax.shard_map(shards, mesh=mesh, in_specs=in_specs, out_specs=out_specs, check_vma=False)
```

```python
import functools

import jax
import jax.numpy as jnp
from jax import lax
from jax.experimental import pallas as pl
from jax.experimental.pallas import tpu as pltpu
from jax.sharding import PartitionSpec as P

D = 8192
FW = 16384
R = 1920
NZ, NX, NY = 8, 4, 4
TOK = 192
ROWS = TOK // NX
epsilon = 1e-06
FACTOR = 0.25 / D
F32 = jnp.float32
BF16 = jnp.bfloat16
MESH = pl.DeviceIdType.MESH


def nn(a, b):
    return lax.dot_general(a, b, (((1,), (0,)), ((), ())), preferred_element_type=F32)


def nt(a, b):
    return lax.dot_general(a, b, (((1,), (1,)), ((), ())), preferred_element_type=F32)


def given(when, act):
    if when is None:
        act()
    else:
        pl.when(when)(act)


class Links:
    def __init__(self, send, recv):
        self.send, self.recv, self.used, self.sent = send, recv, 0, []
        mp, dp = lax.axis_index("mp"), lax.axis_index("dp")
        self.z, self.x = mp // NX, mp % NX
        self.y, self.c = dp // 2, dp % 2

    def at(self, z=None, x=None, y=None, c=None):
        z = self.z if z is None else z
        x = self.x if x is None else x
        y = self.y if y is None else y
        c = self.c if c is None else c
        return (z * NX + x, y * 2 + c)

    def copy(self, src, dst, device, when=None):
        k = self.used
        self.used += 1
        made = pltpu.make_async_remote_copy(
            src_ref=src, dst_ref=dst, send_sem=self.send.at[k], recv_sem=self.recv.at[k],
            device_id=device, device_id_type=MESH)
        given(when, made.start)
        self.sent.append((made, when))
        return made

    def finish(self):
        for made, when in self.sent:
            given(when, made.wait_send)


class AllReduce:
    def __init__(self, net, part, got_x, row, got_z, full, blocks=NZ):
        self.net, self.part, self.got_x, self.row, self.got_z, self.full = net, part, got_x, row, got_z, full
        self.blocks = blocks

    def all(self, ref, i):
        return ref.at[i] if self.blocks == NZ else ref.at[i, pl.ds(0, self.blocks)]

    def keeps(self, z):
        return None if self.blocks == NZ else z % 4 != 3

    def block(self, z):
        return z if self.blocks == NZ else z // 4 * 3 + jnp.minimum(z % 4, 2)

    def scatter_x(self):
        n = self.net
        self.a = [n.copy(self.all(self.part, (n.x + o) % NX), self.all(self.got_x, o - 1), n.at(x=(n.x + o) % NX))
                  for o in range(1, NX)]

    def scatter_z(self):
        n = self.net
        for made in self.a:
            made.wait_recv()

        def add(k, _):
            total = self.part[n.x, k].astype(F32)
            for o in range(NX - 1):
                total = total + self.got_x[o, k].astype(F32)
            self.row[k] = total.astype(BF16)
            return 0
        lax.fori_loop(0, self.blocks, add, 0)
        self.b = []
        for o in range(1, NZ):
            to = (n.z + o) % NZ
            self.b.append(n.copy(self.row.at[self.block(to)], self.got_z.at[o - 1], n.at(z=to), self.keeps(to)))

    def sum_z(self):
        for made in self.b:
            made.wait_recv()
        total = self.row[self.block(self.net.z)].astype(F32)
        for o in range(NZ - 1):
            total = total + self.got_z[o].astype(F32)
        return total

    def gather_z(self):
        n = self.net
        mine = self.block(n.z)

        def settle():
            self.full[n.x, mine] = self.sum_z().astype(BF16)
        given(self.keeps(n.z), settle)
        self.d = [n.copy(self.full.at[n.x, mine], self.full.at[n.x, mine], n.at(z=(n.z + o) % NZ), self.keeps(n.z))
                  for o in range(1, NZ)]

    def gather_x(self):
        n = self.net
        for o, made in enumerate(self.d, 1):
            given(self.keeps((n.z + NZ - o) % NZ), made.wait_recv)
        own = self.all(self.full, n.x)
        self.e = [n.copy(own, own, n.at(x=(n.x + o) % NX)) for o in range(1, NX)]

    def done(self):
        for made in self.e:
            made.wait_recv()


class ScatterZX:
    def __init__(self, net, part, got_z, row, got_x):
        self.net, self.part, self.got_z, self.row, self.got_x = net, part, got_z, row, got_x

    def scatter_z(self):
        n = self.net
        self.a = [n.copy(self.part.at[(n.z + o) % NZ], self.got_z.at[o - 1], n.at(z=(n.z + o) % NZ))
                  for o in range(1, NZ)]

    def scatter_x(self):
        n = self.net
        for made in self.a:
            made.wait_recv()

        def add(k, _):
            total = self.part[n.z, k].astype(F32)
            for o in range(NZ - 1):
                total = total + self.got_z[o, k].astype(F32)
            self.row[k] = total.astype(BF16)
            return 0
        lax.fori_loop(0, NX, add, 0)
        self.b = [n.copy(self.row.at[(n.x + o) % NX], self.got_x.at[o - 1], n.at(x=(n.x + o) % NX))
                  for o in range(1, NX)]

    def sum_x(self):
        for made in self.b:
            made.wait_recv()
        total = self.row[self.net.x].astype(F32)
        for o in range(NX - 1):
            total = total + self.got_x[o].astype(F32)
        return total


class GatherDp:
    def __init__(self, net, part):
        self.net, self.part = net, part

    def start(self, src=None):
        n = self.net
        d = n.y * 2 + n.c
        own = self.part(d, None)
        src = own if src is None else src
        self.up = n.copy(src, own, n.at(y=(n.y + 1) % NY))
        self.down = n.copy(src, own, n.at(y=(n.y + NY - 1) % NY))
        self.over = [n.copy(src, own, n.at(c=1 - n.c))]

    def relay(self):
        n = self.net
        below = ((n.y + NY - 1) % NY) * 2 + n.c
        above = ((n.y + 1) % NY) * 2 + n.c
        self.up.wait_recv()
        self.up2 = n.copy(self.part(below, 0), self.part(below, 0), n.at(y=(n.y + 1) % NY))
        self.over.append(n.copy(self.part(below, None), self.part(below, None), n.at(c=1 - n.c)))
        self.down.wait_recv()
        self.down2 = n.copy(self.part(above, 1), self.part(above, 1), n.at(y=(n.y + NY - 1) % NY))
        self.over.append(n.copy(self.part(above, None), self.part(above, None), n.at(c=1 - n.c)))

    def relay_far(self):
        n = self.net
        far = ((n.y + 2) % NY) * 2 + n.c
        self.up2.wait_recv()
        self.over.append(n.copy(self.part(far, 0), self.part(far, 0), n.at(c=1 - n.c)))
        self.down2.wait_recv()
        self.over.append(n.copy(self.part(far, 1), self.part(far, 1), n.at(c=1 - n.c)))

    def done(self):
        for made in self.over:
            made.wait_recv()


class GatherMp:
    def __init__(self, net, block):
        self.net, self.block = net, block

    def start(self):
        n = self.net
        own = self.block.at[n.z, n.x]
        self.a = [n.copy(own, own, n.at(x=(n.x + o) % NX)) for o in range(1, NX)]
        self.s = 0

    def step(self):
        n, s = self.net, self.s
        if s == 0:
            for made in self.a:
                made.wait_recv()
        else:
            self.up.wait_recv()
            if s <= NZ // 2 - 1:
                self.down.wait_recv()
        if s < NZ // 2:
            up = self.block.at[(n.z + NZ - s) % NZ]
            self.up = n.copy(up, up, n.at(z=(n.z + 1) % NZ))
        if s < NZ // 2 - 1:
            down = self.block.at[(n.z + s) % NZ]
            self.down = n.copy(down, down, n.at(z=(n.z + NZ - 1) % NZ))
        self.s += 1


def body(x_hbm, g_hbm, w_hbm, ei_hbm, di_hbm, eo_hbm, do_hbm, post_ref, gin_ref,
         xin, g, w, ei, di, eo, do, part, got_x, row, got_z, full, edits, grads, total, cot,
         bpart, bgot_x, brow, bgot_z, zpart, zgot_z, zrow, zgot_x, send, recv, load):
    net = Links(send, recv)
    z, x, y, c = net.z, net.x, net.y, net.c
    d = y * 2 + c

    loads = []
    for k, (src, dst) in enumerate(((x_hbm, xin.at[z, x]), (ei_hbm, ei), (g_hbm, g), (eo_hbm, eo),
                                    (di_hbm, di), (do_hbm, do), (w_hbm, w.at[d]))):
        made = pltpu.make_async_copy(src, dst, load.at[k])
        made.start()
        loads.append(made)

    barrier = pltpu.get_barrier_semaphore()
    peers = ([net.at(x=(x + o) % NX) for o in range(1, NX)] + [net.at(z=(z + o) % NZ) for o in range(1, NZ)]
             + [net.at(y=(y + 1) % NY), net.at(y=(y + NY - 1) % NY), net.at(c=1 - c)])
    for peer in peers:
        pl.semaphore_signal(barrier, inc=1, device_id=peer, device_id_type=MESH)
    pl.semaphore_wait(barrier, len(peers))

    def w_part(slot, half):
        return w.at[slot] if half is None else w.at[slot, pl.ds(2 * half, 2)]

    def rows_of(ref):
        def pick(slot, half):
            count = TOK if half is None else TOK // 2
            return ref.at[pl.ds(pl.multiple_of(slot * TOK + (half or 0) * count, 32), count)]
        return pick

    whole_w = GatherDp(net, w_part)
    whole_w.start(w_hbm)
    loads[0].wait()
    whole_in = GatherMp(net, xin)
    whole_in.start()

    own = xin[z, x]

    def project(value, enc, out):
        for k in range(7):
            block = nn(value, enc[:, 256 * k:256 * k + 256])
            out[:, k] = block.astype(BF16).reshape(NX, ROWS, 256)
        last = nn(value, enc[:, 1792:1920])
        out[:, 7, :, 0:128] = last.astype(BF16).reshape(NX, ROWS, 128)
        wide = value.astype(F32)
        square = wide * wide
        fold = square[:, 0:128]
        for k in range(1, value.shape[1] // 128):
            fold = fold + square[:, 128 * k:128 * k + 128]
        out[:, 7, :, 128:256] = fold.astype(BF16).reshape(NX, ROWS, 128)

    reduce_in, reduce_out, reduce_kernel, reduce_back = [
        AllReduce(net, part.at[k], got_x.at[k], row.at[k], got_z.at[k], full.at[k], 8 if k < 2 else 6)
        for k in range(4)]

    loads[1].wait()
    project(own, ei, part.at[0])
    reduce_in.scatter_x()
    loads[2].wait()
    loads[3].wait()
    project(g[...], eo, part.at[1])
    total[...] = jnp.zeros_like(total)
    for made in loads[4:]:
        made.wait()
    whole_in.step()
    reduce_in.scatter_z()
    reduce_out.scatter_x()
    reduce_in.gather_z()
    reduce_in.gather_x()
    whole_in.step()
    reduce_out.scatter_z()
    reduce_out.gather_z()
    whole_w.relay()

    def edit(value, hidden, dec, features):
        squares = hidden[:, 7, :, 128:256].astype(F32).reshape(TOK, 128)
        scale = lax.rsqrt(jnp.sum(squares, axis=1, keepdims=True) / features + epsilon)
        out = value.astype(F32)
        for k in range(8):
            width = 256 if k < 7 else 128
            h = hidden[:, k, :, 0:width].astype(F32).reshape(TOK, width)
            h = jnp.maximum(h * scale, 0.0).astype(BF16)
            out = out + nn(h, dec[256 * k:256 * k + width, :])
        return out.astype(BF16)

    gather_edits = GatherDp(net, rows_of(edits))
    gather_grads = GatherDp(net, rows_of(grads))
    reduce_in.done()
    rows_own = pl.ds(pl.multiple_of(d * TOK, 64), TOK)
    edits[rows_own, :] = edit(own, full.at[0], di, D)
    gather_edits.start()
    reduce_out.gather_x()
    gather_edits.relay()
    gather_edits.relay_far()
    gather_edits.done()

    def inner(k, _):
        part[2, :, k] = nt(own, edits[pl.ds(pl.multiple_of(k * 256, 256), 256), :]).astype(BF16).reshape(NX, ROWS, 256)
        return 0
    lax.fori_loop(0, 6, inner, 0)
    reduce_kernel.scatter_x()
    whole_in.step()
    reduce_out.done()
    grads[rows_own, :] = edit(g[...], full.at[1], do, FW)
    gather_grads.start()
    reduce_kernel.scatter_z()
    gather_grads.relay()
    whole_w.relay_far()
    reduce_kernel.gather_z()
    whole_in.step()
    gather_grads.relay_far()
    reduce_kernel.gather_x()
    whole_w.done()
    whole_in.step()

    def base(k, _):
        value = nn(xin[k, 0], w[k, 0])
        for j in range(1, NX):
            value = value + nn(xin[k, j], w[k, j])
        total[...] += value
        return 0
    lax.fori_loop(0, NZ, base, 0)
    gather_grads.done()
    reduce_kernel.done()

    def correct(k, _):
        block = (full[2, :, k].astype(F32) * FACTOR).astype(BF16).reshape(TOK, 256)
        total[...] -= nn(block, grads[pl.ds(pl.multiple_of(k * 256, 256), 256), :])
        return 0
    lax.fori_loop(0, 6, correct, 0)

    def activate(k, _):
        rows = pl.ds(k * ROWS, ROWS)
        post = total[rows, :]
        post_ref[rows, :] = post.astype(BF16)
        sig = jax.nn.sigmoid(post)
        cot[rows, :] = (g[rows, :].astype(F32) * (sig * (1.0 + post * (1.0 - sig)))).astype(BF16)
        return 0
    lax.fori_loop(0, NX, activate, 0)

    def back_inner(k, _):
        some = grads[pl.ds(pl.multiple_of(k * 256, 256), 256), :]
        part[3, :, k] = nt(cot[...], some).astype(BF16).reshape(NX, ROWS, 256)
        return 0
    lax.fori_loop(0, 6, back_inner, 0)
    reduce_back.scatter_x()

    def back_block(k, _):
        for j in range(NX):
            value = nt(cot[...], w[k, j]).astype(BF16).reshape(NX, ROWS, 256)
            for p in range(3):
                bpart[p, j, k] = value[p]
            zpart[k, j] = value[3]
        return 0
    lax.fori_loop(0, NZ, back_block, 0)
    pieces = [AllReduce(net, bpart.at[p], bgot_x.at[p], brow.at[p], bgot_z.at[p], None) for p in range(3)]
    last = ScatterZX(net, zpart, zgot_z, zrow, zgot_x)
    last.scatter_z()
    pieces[0].scatter_x()
    reduce_back.scatter_z()
    pieces[1].scatter_x()
    reduce_back.gather_z()
    pieces[2].scatter_x()
    pieces[0].scatter_z()
    reduce_back.gather_x()
    last.scatter_x()
    pieces[1].scatter_z()
    pieces[2].scatter_z()
    reduce_back.done()
    result = jnp.zeros((TOK, 256), F32)
    for k in range(6):
        block = (full[3, :, k].astype(F32) * FACTOR).astype(BF16).reshape(TOK, 256)
        result = result - nn(block, edits[256 * k:256 * k + 256, :])
    sums = [last.sum_x()]
    sums = [piece.sum_z() for piece in pieces] + sums
    for p in range(NX):
        rows = slice(ROWS * p, ROWS * p + ROWS)
        gin_ref[rows, :] = (result[rows] + sums[p]).astype(BF16)

    net.finish()


COPIES = 160


def shards(inputs, out_grads, weight, enc_in, dec_in, enc_out, dec_out):
    anywhere = pl.BlockSpec(memory_space=pl.ANY)
    vmem = pl.BlockSpec(memory_space=pltpu.VMEM)
    scratch = [
        pltpu.VMEM((NZ, NX, TOK, 256), BF16),
        pltpu.VMEM((TOK, 512), BF16),
        pltpu.VMEM((8, 4, 256, 512), BF16),
        pltpu.VMEM((256, R), BF16),
        pltpu.VMEM((R, 256), BF16),
        pltpu.VMEM((512, R), BF16),
        pltpu.VMEM((R, 512), BF16),
        pltpu.VMEM((4, NX, NZ, ROWS, 256), BF16),
        pltpu.VMEM((4, NX - 1, NZ, ROWS, 256), BF16),
        pltpu.VMEM((4, NZ, ROWS, 256), BF16),
        pltpu.VMEM((4, NZ - 1, ROWS, 256), BF16),
        pltpu.VMEM((4, NX, NZ, ROWS, 256), BF16),
        pltpu.VMEM((8 * TOK, 256), BF16),
        pltpu.VMEM((8 * TOK, 512), BF16),
        pltpu.VMEM((TOK, 512), F32),
        pltpu.VMEM((TOK, 512), BF16),
        pltpu.VMEM((3, NX, NZ, ROWS, 256), BF16),
        pltpu.VMEM((3, NX - 1, NZ, ROWS, 256), BF16),
        pltpu.VMEM((3, NZ, ROWS, 256), BF16),
        pltpu.VMEM((3, NZ - 1, ROWS, 256), BF16),
        pltpu.VMEM((NZ, NX, ROWS, 256), BF16),
        pltpu.VMEM((NZ - 1, NX, ROWS, 256), BF16),
        pltpu.VMEM((NX, ROWS, 256), BF16),
        pltpu.VMEM((NX - 1, ROWS, 256), BF16),
        pltpu.SemaphoreType.DMA((COPIES,)),
        pltpu.SemaphoreType.DMA((COPIES,)),
        pltpu.SemaphoreType.DMA((7,)),
    ]
    return pl.pallas_call(
        body,
        out_shape=(jax.ShapeDtypeStruct((TOK, 512), BF16), jax.ShapeDtypeStruct((TOK, 256), BF16)),
        in_specs=[anywhere] * 7,
        out_specs=(vmem, vmem),
        scratch_shapes=scratch,
        compiler_params=pltpu.CompilerParams(
            collective_id=0, has_side_effects=True, vmem_limit_bytes=60 * 1024 * 1024),
    )(inputs, out_grads, weight.reshape(4, 256, 512), enc_in, dec_in, enc_out, dec_out)


def solution(mesh):
    in_specs = (
        P("dp", "mp"),
        P("dp", "mp"),
        P("dp", "mp"),
        P("mp", None),
        P(None, "mp"),
        P("mp", None),
        P(None, "mp"),
    )
    out_specs = (P("dp", "mp"), P("dp", "mp"))
    return jax.shard_map(shards, mesh=mesh, in_specs=in_specs, out_specs=out_specs, check_vma=False)
```

```python
import functools

import jax
import jax.numpy as jnp
from jax import lax
from jax.experimental import pallas as pl
from jax.experimental.pallas import tpu as pltpu
from jax.sharding import PartitionSpec as P

D = 8192
FW = 16384
R = 1920
NZ, NX, NY = 8, 4, 4
TOK = 192
ROWS = TOK // NX
epsilon = 1e-06
FACTOR = 0.25 / D
F32 = jnp.float32
BF16 = jnp.bfloat16
MESH = pl.DeviceIdType.MESH


def nn(a, b):
    return lax.dot_general(a, b, (((1,), (0,)), ((), ())), preferred_element_type=F32)


def nt(a, b):
    return lax.dot_general(a, b, (((1,), (1,)), ((), ())), preferred_element_type=F32)


def given(when, act):
    if when is None:
        act()
    else:
        pl.when(when)(act)


class Links:
    def __init__(self, send, recv):
        self.send, self.recv, self.used, self.sent = send, recv, 0, []
        mp, dp = lax.axis_index("mp"), lax.axis_index("dp")
        self.z, self.x = mp // NX, mp % NX
        self.y, self.c = dp // 2, dp % 2

    def at(self, z=None, x=None, y=None, c=None):
        z = self.z if z is None else z
        x = self.x if x is None else x
        y = self.y if y is None else y
        c = self.c if c is None else c
        return (z * NX + x, y * 2 + c)

    def copy(self, src, dst, device, when=None):
        k = self.used
        self.used += 1
        made = pltpu.make_async_remote_copy(
            src_ref=src, dst_ref=dst, send_sem=self.send.at[k], recv_sem=self.recv.at[k],
            device_id=device, device_id_type=MESH)
        given(when, made.start)
        self.sent.append((made, when))
        return made

    def finish(self):
        for made, when in self.sent:
            given(when, made.wait_send)


class AllReduce:
    def __init__(self, net, part, got_x, row, got_z, full, blocks=NZ):
        self.net, self.part, self.got_x, self.row, self.got_z, self.full = net, part, got_x, row, got_z, full
        self.blocks = blocks

    def all(self, ref, i):
        return ref.at[i] if self.blocks == NZ else ref.at[i, pl.ds(0, self.blocks)]

    def keeps(self, z):
        return None if self.blocks == NZ else z % 4 != 3

    def block(self, z):
        return z if self.blocks == NZ else z // 4 * 3 + jnp.minimum(z % 4, 2)

    def scatter_x(self):
        n = self.net
        self.a = [n.copy(self.all(self.part, (n.x + o) % NX), self.all(self.got_x, o - 1), n.at(x=(n.x + o) % NX))
                  for o in range(1, NX)]

    def scatter_z(self):
        n = self.net
        for made in self.a:
            made.wait_recv()

        def add(k, _):
            total = self.part[n.x, k].astype(F32)
            for o in range(NX - 1):
                total = total + self.got_x[o, k].astype(F32)
            self.row[k] = total.astype(BF16)
            return 0
        lax.fori_loop(0, self.blocks, add, 0)
        self.b = []
        for o in range(1, NZ):
            to = (n.z + o) % NZ
            self.b.append(n.copy(self.row.at[self.block(to)], self.got_z.at[o - 1], n.at(z=to), self.keeps(to)))

    def sum_z(self):
        for made in self.b:
            made.wait_recv()
        total = self.row[self.block(self.net.z)].astype(F32)
        for o in range(NZ - 1):
            total = total + self.got_z[o].astype(F32)
        return total

    def gather_z(self):
        n = self.net
        mine = self.block(n.z)

        def settle():
            self.full[n.x, mine] = self.sum_z().astype(BF16)
        given(self.keeps(n.z), settle)
        self.d = [n.copy(self.full.at[n.x, mine], self.full.at[n.x, mine], n.at(z=(n.z + o) % NZ), self.keeps(n.z))
                  for o in range(1, NZ)]

    def gather_x(self):
        n = self.net
        for o, made in enumerate(self.d, 1):
            given(self.keeps((n.z + NZ - o) % NZ), made.wait_recv)
        own = self.all(self.full, n.x)
        self.e = [n.copy(own, own, n.at(x=(n.x + o) % NX)) for o in range(1, NX)]

    def done(self):
        for made in self.e:
            made.wait_recv()


class ScatterZX:
    def __init__(self, net, part, got_z, row, got_x):
        self.net, self.part, self.got_z, self.row, self.got_x = net, part, got_z, row, got_x

    def scatter_z(self):
        n = self.net
        self.a = [n.copy(self.part.at[(n.z + o) % NZ], self.got_z.at[o - 1], n.at(z=(n.z + o) % NZ))
                  for o in range(1, NZ)]

    def scatter_x(self):
        n = self.net
        for made in self.a:
            made.wait_recv()

        def add(k, _):
            total = self.part[n.z, k].astype(F32)
            for o in range(NZ - 1):
                total = total + self.got_z[o, k].astype(F32)
            self.row[k] = total.astype(BF16)
            return 0
        lax.fori_loop(0, NX, add, 0)
        self.b = [n.copy(self.row.at[(n.x + o) % NX], self.got_x.at[o - 1], n.at(x=(n.x + o) % NX))
                  for o in range(1, NX)]

    def sum_x(self):
        for made in self.b:
            made.wait_recv()
        total = self.row[self.net.x].astype(F32)
        for o in range(NX - 1):
            total = total + self.got_x[o].astype(F32)
        return total


class GatherDp:
    def __init__(self, net, part):
        self.net, self.part = net, part

    def start(self, src=None):
        n = self.net
        d = n.y * 2 + n.c
        own = self.part(d, None)
        src = own if src is None else src
        self.up = n.copy(src, own, n.at(y=(n.y + 1) % NY))
        self.down = n.copy(src, own, n.at(y=(n.y + NY - 1) % NY))
        self.over = [n.copy(src, own, n.at(c=1 - n.c))]

    def relay(self):
        n = self.net
        below = ((n.y + NY - 1) % NY) * 2 + n.c
        above = ((n.y + 1) % NY) * 2 + n.c
        self.up.wait_recv()
        self.up2 = n.copy(self.part(below, 0), self.part(below, 0), n.at(y=(n.y + 1) % NY))
        self.over.append(n.copy(self.part(below, None), self.part(below, None), n.at(c=1 - n.c)))
        self.down.wait_recv()
        self.down2 = n.copy(self.part(above, 1), self.part(above, 1), n.at(y=(n.y + NY - 1) % NY))
        self.over.append(n.copy(self.part(above, None), self.part(above, None), n.at(c=1 - n.c)))

    def relay_far(self):
        n = self.net
        far = ((n.y + 2) % NY) * 2 + n.c
        self.up2.wait_recv()
        self.over.append(n.copy(self.part(far, 0), self.part(far, 0), n.at(c=1 - n.c)))
        self.down2.wait_recv()
        self.over.append(n.copy(self.part(far, 1), self.part(far, 1), n.at(c=1 - n.c)))

    def done(self):
        for made in self.over:
            made.wait_recv()


class GatherNear:
    def __init__(self, net, part):
        self.net, self.part = net, part

    def start(self):
        n = self.net
        own = self.part(n.y * 2 + n.c, None)
        self.near = [n.copy(own, own, n.at(y=(n.y + o) % NY)) for o in (1, 3, 2)]
        self.over = [n.copy(own, own, n.at(c=1 - n.c))]

    def relay(self):
        n = self.net
        for o, made in zip((1, 3, 2), self.near):
            made.wait_recv()
            slot = self.part((n.y + NY - o) % NY * 2 + n.c, None)
            self.over.append(n.copy(slot, slot, n.at(c=1 - n.c)))

    def done(self):
        for made in self.over:
            made.wait_recv()


class GatherMp:
    def __init__(self, net, block):
        self.net, self.block = net, block

    def start(self):
        n = self.net
        own = self.block.at[n.z, n.x]
        self.a = [n.copy(own, own, n.at(x=(n.x + o) % NX)) for o in range(1, NX)]
        self.s = 0

    def step(self):
        n, s = self.net, self.s
        if s == 0:
            for made in self.a:
                made.wait_recv()
        else:
            self.up.wait_recv()
            if s <= NZ // 2 - 1:
                self.down.wait_recv()
        if s < NZ // 2:
            up = self.block.at[(n.z + NZ - s) % NZ]
            self.up = n.copy(up, up, n.at(z=(n.z + 1) % NZ))
        if s < NZ // 2 - 1:
            down = self.block.at[(n.z + s) % NZ]
            self.down = n.copy(down, down, n.at(z=(n.z + NZ - 1) % NZ))
        self.s += 1


def body(x_hbm, g_hbm, w_hbm, ei_hbm, di_hbm, eo_hbm, do_hbm, post_ref, gin_ref,
         xin, g, w, ei, di, eo, do, part, got_x, row, got_z, full, edits, grads, total, cot,
         bpart, bgot_x, brow, bgot_z, zpart, zgot_z, zrow, zgot_x, send, recv, load):
    net = Links(send, recv)
    z, x, y, c = net.z, net.x, net.y, net.c
    d = y * 2 + c

    loads = []
    for k, (src, dst) in enumerate(((x_hbm, xin.at[z, x]), (ei_hbm, ei), (g_hbm, g), (eo_hbm, eo),
                                    (di_hbm, di), (do_hbm, do), (w_hbm, w.at[d]))):
        made = pltpu.make_async_copy(src, dst, load.at[k])
        made.start()
        loads.append(made)

    barrier = pltpu.get_barrier_semaphore()
    peers = ([net.at(x=(x + o) % NX) for o in range(1, NX)] + [net.at(z=(z + o) % NZ) for o in range(1, NZ)]
             + [net.at(y=(y + o) % NY) for o in range(1, NY)] + [net.at(c=1 - c)])
    for peer in peers:
        pl.semaphore_signal(barrier, inc=1, device_id=peer, device_id_type=MESH)

    def w_part(slot, half):
        return w.at[slot] if half is None else w.at[slot, pl.ds(2 * half, 2)]

    def rows_of(ref):
        def pick(slot, half):
            count = TOK if half is None else TOK // 2
            return ref.at[pl.ds(pl.multiple_of(slot * TOK + (half or 0) * count, 32), count)]
        return pick

    whole_w = GatherDp(net, w_part)
    whole_in = GatherMp(net, xin)
    loads[0].wait()
    own = xin[z, x]

    def project(value, enc, out):
        for k in range(7):
            block = nn(value, enc[:, 256 * k:256 * k + 256])
            out[:, k] = block.astype(BF16).reshape(NX, ROWS, 256)
        last = nn(value, enc[:, 1792:1920])
        out[:, 7, :, 0:128] = last.astype(BF16).reshape(NX, ROWS, 128)
        wide = value.astype(F32)
        square = wide * wide
        fold = square[:, 0:128]
        for k in range(1, value.shape[1] // 128):
            fold = fold + square[:, 128 * k:128 * k + 128]
        out[:, 7, :, 128:256] = fold.astype(BF16).reshape(NX, ROWS, 128)

    reduce_in, reduce_out, reduce_kernel, reduce_back = [
        AllReduce(net, part.at[k], got_x.at[k], row.at[k], got_z.at[k], full.at[k], 8 if k < 2 else 6)
        for k in range(4)]

    loads[1].wait()
    project(own, ei, part.at[0])
    pl.semaphore_wait(barrier, len(peers))
    reduce_in.scatter_x()
    whole_w.start(w_hbm)
    loads[2].wait()
    loads[3].wait()
    project(g[...], eo, part.at[1])
    total[...] = jnp.zeros_like(total)
    for made in loads[4:]:
        made.wait()
    reduce_in.scatter_z()
    reduce_out.scatter_x()
    whole_in.start()
    reduce_in.gather_z()
    reduce_in.gather_x()
    whole_in.step()
    reduce_out.scatter_z()

    def edit(value, hidden, dec, features):
        squares = hidden[:, 7, :, 128:256].astype(F32).reshape(TOK, 128)
        scale = lax.rsqrt(jnp.sum(squares, axis=1, keepdims=True) / features + epsilon)
        out = value.astype(F32)
        for k in range(8):
            width = 256 if k < 7 else 128
            h = hidden[:, k, :, 0:width].astype(F32).reshape(TOK, width)
            h = jnp.maximum(h * scale, 0.0).astype(BF16)
            out = out + nn(h, dec[256 * k:256 * k + width, :])
        return out.astype(BF16)

    gather_edits = GatherNear(net, rows_of(edits))
    gather_grads = GatherNear(net, rows_of(grads))
    reduce_in.done()
    rows_own = pl.ds(pl.multiple_of(d * TOK, 64), TOK)
    edits[rows_own, :] = edit(own, full.at[0], di, D)
    gather_edits.start()
    reduce_out.gather_z()
    gather_edits.relay()
    gather_edits.done()

    def inner(k, _):
        some = edits[pl.ds(pl.multiple_of(k * 256, 256), 256), :]
        part[2, :, k] = nt(own, some).astype(BF16).reshape(NX, ROWS, 256)
        return 0
    lax.fori_loop(0, 6, inner, 0)
    reduce_kernel.scatter_x()
    whole_in.step()
    reduce_out.gather_x()
    whole_w.relay()
    reduce_kernel.scatter_z()
    whole_in.step()
    reduce_out.done()
    grads[rows_own, :] = edit(g[...], full.at[1], do, FW)
    gather_grads.start()
    reduce_kernel.gather_z()
    whole_in.step()
    whole_w.relay_far()
    gather_grads.relay()
    reduce_kernel.gather_x()
    whole_in.step()
    whole_w.done()

    def base(k, _):
        value = nn(xin[k, 0], w[k, 0])
        for j in range(1, NX):
            value = value + nn(xin[k, j], w[k, j])
        total[...] += value
        return 0
    lax.fori_loop(0, NZ, base, 0)
    gather_grads.done()
    reduce_kernel.done()

    def correct(k, _):
        block = (full[2, :, k].astype(F32) * FACTOR).astype(BF16).reshape(TOK, 256)
        total[...] -= nn(block, grads[pl.ds(pl.multiple_of(k * 256, 256), 256), :])
        return 0
    lax.fori_loop(0, 6, correct, 0)

    def activate(k, _):
        rows = pl.ds(k * ROWS, ROWS)
        post = total[rows, :]
        post_ref[rows, :] = post.astype(BF16)
        sig = jax.nn.sigmoid(post)
        cot[rows, :] = (g[rows, :].astype(F32) * (sig * (1.0 + post * (1.0 - sig)))).astype(BF16)
        return 0
    lax.fori_loop(0, NX, activate, 0)

    def back_inner(k, _):
        some = grads[pl.ds(pl.multiple_of(k * 256, 256), 256), :]
        part[3, :, k] = nt(cot[...], some).astype(BF16).reshape(NX, ROWS, 256)
        return 0
    lax.fori_loop(0, 6, back_inner, 0)
    reduce_back.scatter_x()

    def back_block(k, _):
        for j in range(NX):
            value = nt(cot[...], w[k, j]).astype(BF16).reshape(NX, ROWS, 256)
            for p in range(3):
                bpart[p, j, k] = value[p]
            zpart[k, j] = value[3]
        return 0
    lax.fori_loop(0, NZ, back_block, 0)
    pieces = [AllReduce(net, bpart.at[p], bgot_x.at[p], brow.at[p], bgot_z.at[p], None) for p in range(3)]
    last = ScatterZX(net, zpart, zgot_z, zrow, zgot_x)
    last.scatter_z()
    pieces[0].scatter_x()
    reduce_back.scatter_z()
    pieces[1].scatter_x()
    reduce_back.gather_z()
    pieces[2].scatter_x()
    pieces[0].scatter_z()
    reduce_back.gather_x()
    last.scatter_x()
    pieces[1].scatter_z()
    pieces[2].scatter_z()
    reduce_back.done()
    result = jnp.zeros((TOK, 256), F32)
    for k in range(6):
        block = (full[3, :, k].astype(F32) * FACTOR).astype(BF16).reshape(TOK, 256)
        result = result - nn(block, edits[256 * k:256 * k + 256, :])
    sums = [last.sum_x()]
    sums = [piece.sum_z() for piece in pieces] + sums
    for p in range(NX):
        rows = slice(ROWS * p, ROWS * p + ROWS)
        gin_ref[rows, :] = (result[rows] + sums[p]).astype(BF16)

    net.finish()


COPIES = 176


def shards(inputs, out_grads, weight, enc_in, dec_in, enc_out, dec_out):
    anywhere = pl.BlockSpec(memory_space=pl.ANY)
    vmem = pl.BlockSpec(memory_space=pltpu.VMEM)
    scratch = [
        pltpu.VMEM((NZ, NX, TOK, 256), BF16),
        pltpu.VMEM((TOK, 512), BF16),
        pltpu.VMEM((8, 4, 256, 512), BF16),
        pltpu.VMEM((256, R), BF16),
        pltpu.VMEM((R, 256), BF16),
        pltpu.VMEM((512, R), BF16),
        pltpu.VMEM((R, 512), BF16),
        pltpu.VMEM((4, NX, NZ, ROWS, 256), BF16),
        pltpu.VMEM((4, NX - 1, NZ, ROWS, 256), BF16),
        pltpu.VMEM((4, NZ, ROWS, 256), BF16),
        pltpu.VMEM((4, NZ - 1, ROWS, 256), BF16),
        pltpu.VMEM((4, NX, NZ, ROWS, 256), BF16),
        pltpu.VMEM((8 * TOK, 256), BF16),
        pltpu.VMEM((8 * TOK, 512), BF16),
        pltpu.VMEM((TOK, 512), F32),
        pltpu.VMEM((TOK, 512), BF16),
        pltpu.VMEM((3, NX, NZ, ROWS, 256), BF16),
        pltpu.VMEM((3, NX - 1, NZ, ROWS, 256), BF16),
        pltpu.VMEM((3, NZ, ROWS, 256), BF16),
        pltpu.VMEM((3, NZ - 1, ROWS, 256), BF16),
        pltpu.VMEM((NZ, NX, ROWS, 256), BF16),
        pltpu.VMEM((NZ - 1, NX, ROWS, 256), BF16),
        pltpu.VMEM((NX, ROWS, 256), BF16),
        pltpu.VMEM((NX - 1, ROWS, 256), BF16),
        pltpu.SemaphoreType.DMA((COPIES,)),
        pltpu.SemaphoreType.DMA((COPIES,)),
        pltpu.SemaphoreType.DMA((7,)),
    ]
    return pl.pallas_call(
        body,
        out_shape=(jax.ShapeDtypeStruct((TOK, 512), BF16), jax.ShapeDtypeStruct((TOK, 256), BF16)),
        in_specs=[anywhere] * 7,
        out_specs=(vmem, vmem),
        scratch_shapes=scratch,
        compiler_params=pltpu.CompilerParams(
            collective_id=0, has_side_effects=True, vmem_limit_bytes=60 * 1024 * 1024),
    )(inputs, out_grads, weight.reshape(4, 256, 512), enc_in, dec_in, enc_out, dec_out)


def solution(mesh):
    in_specs = (
        P("dp", "mp"),
        P("dp", "mp"),
        P("dp", "mp"),
        P("mp", None),
        P(None, "mp"),
        P("mp", None),
        P(None, "mp"),
    )
    out_specs = (P("dp", "mp"), P("dp", "mp"))
    return jax.shard_map(shards, mesh=mesh, in_specs=in_specs, out_specs=out_specs, check_vma=False)
```

```python
import functools

import jax
import jax.numpy as jnp
from jax import lax
from jax.experimental import pallas as pl
from jax.experimental.pallas import tpu as pltpu
from jax.sharding import PartitionSpec as P

D = 8192
FW = 16384
R = 1920
NZ, NX, NY = 8, 4, 4
TOK = 192
ROWS = TOK // NX
epsilon = 1e-06
FACTOR = 0.25 / D
F32 = jnp.float32
BF16 = jnp.bfloat16
MESH = pl.DeviceIdType.MESH


def nn(a, b):
    return lax.dot_general(a, b, (((1,), (0,)), ((), ())), preferred_element_type=F32)


def nt(a, b):
    return lax.dot_general(a, b, (((1,), (1,)), ((), ())), preferred_element_type=F32)


def given(when, act):
    if when is None:
        act()
    else:
        pl.when(when)(act)


class Links:
    def __init__(self, send, recv):
        self.send, self.recv, self.used, self.sent = send, recv, 0, []
        mp, dp = lax.axis_index("mp"), lax.axis_index("dp")
        self.z, self.x = mp // NX, mp % NX
        self.y, self.c = dp // 2, dp % 2

    def at(self, z=None, x=None, y=None, c=None):
        z = self.z if z is None else z
        x = self.x if x is None else x
        y = self.y if y is None else y
        c = self.c if c is None else c
        return (z * NX + x, y * 2 + c)

    def copy(self, src, dst, device, when=None):
        k = self.used
        self.used += 1
        made = pltpu.make_async_remote_copy(
            src_ref=src, dst_ref=dst, send_sem=self.send.at[k], recv_sem=self.recv.at[k],
            device_id=device, device_id_type=MESH)
        given(when, made.start)
        self.sent.append((made, when))
        return made

    def finish(self):
        for made, when in self.sent:
            given(when, made.wait_send)


class AllReduce:
    def __init__(self, net, part, got_x, row, got_z, full, blocks=NZ):
        self.net, self.part, self.got_x, self.row, self.got_z, self.full = net, part, got_x, row, got_z, full
        self.blocks = blocks

    def all(self, ref, i):
        return ref.at[i] if self.blocks == NZ else ref.at[i, pl.ds(0, self.blocks)]

    def keeps(self, z):
        return None if self.blocks == NZ else z % 4 != 3

    def block(self, z):
        return z if self.blocks == NZ else z // 4 * 3 + jnp.minimum(z % 4, 2)

    def scatter_x(self):
        n = self.net
        self.a = [n.copy(self.all(self.part, (n.x + o) % NX), self.all(self.got_x, o - 1), n.at(x=(n.x + o) % NX))
                  for o in range(1, NX)]

    def scatter_z(self):
        n = self.net
        for made in self.a:
            made.wait_recv()

        def add(k, _):
            total = self.part[n.x, k].astype(F32)
            for o in range(NX - 1):
                total = total + self.got_x[o, k].astype(F32)
            self.row[k] = total.astype(BF16)
            return 0
        lax.fori_loop(0, self.blocks, add, 0)
        self.b = []
        for o in range(1, NZ):
            to = (n.z + o) % NZ
            self.b.append(n.copy(self.row.at[self.block(to)], self.got_z.at[o - 1], n.at(z=to), self.keeps(to)))

    def sum_z(self):
        for made in self.b:
            made.wait_recv()
        total = self.row[self.block(self.net.z)].astype(F32)
        for o in range(NZ - 1):
            total = total + self.got_z[o].astype(F32)
        return total

    def gather_z(self):
        n = self.net
        mine = self.block(n.z)

        def settle():
            self.full[n.x, mine] = self.sum_z().astype(BF16)
        given(self.keeps(n.z), settle)
        self.d = [n.copy(self.full.at[n.x, mine], self.full.at[n.x, mine], n.at(z=(n.z + o) % NZ), self.keeps(n.z))
                  for o in range(1, NZ)]

    def gather_x(self):
        n = self.net
        for o, made in enumerate(self.d, 1):
            given(self.keeps((n.z + NZ - o) % NZ), made.wait_recv)
        own = self.all(self.full, n.x)
        self.e = [n.copy(own, own, n.at(x=(n.x + o) % NX)) for o in range(1, NX)]

    def done(self):
        for made in self.e:
            made.wait_recv()


class ScatterZX:
    def __init__(self, net, part, got_z, row, got_x):
        self.net, self.part, self.got_z, self.row, self.got_x = net, part, got_z, row, got_x

    def scatter_z(self):
        n = self.net
        self.a = [n.copy(self.part.at[(n.z + o) % NZ], self.got_z.at[o - 1], n.at(z=(n.z + o) % NZ))
                  for o in range(1, NZ)]

    def scatter_x(self):
        n = self.net
        for made in self.a:
            made.wait_recv()

        def add(k, _):
            total = self.part[n.z, k].astype(F32)
            for o in range(NZ - 1):
                total = total + self.got_z[o, k].astype(F32)
            self.row[k] = total.astype(BF16)
            return 0
        lax.fori_loop(0, NX, add, 0)
        self.b = [n.copy(self.row.at[(n.x + o) % NX], self.got_x.at[o - 1], n.at(x=(n.x + o) % NX))
                  for o in range(1, NX)]

    def sum_x(self):
        for made in self.b:
            made.wait_recv()
        total = self.row[self.net.x].astype(F32)
        for o in range(NX - 1):
            total = total + self.got_x[o].astype(F32)
        return total


class GatherDp:
    def __init__(self, net, part):
        self.net, self.part = net, part

    def start(self, src=None):
        n = self.net
        d = n.y * 2 + n.c
        own = self.part(d, None)
        src = own if src is None else src
        self.up = n.copy(src, own, n.at(y=(n.y + 1) % NY))
        self.down = n.copy(src, own, n.at(y=(n.y + NY - 1) % NY))
        self.over = [n.copy(src, own, n.at(c=1 - n.c))]

    def relay(self):
        n = self.net
        below = ((n.y + NY - 1) % NY) * 2 + n.c
        above = ((n.y + 1) % NY) * 2 + n.c
        self.up.wait_recv()
        self.up2 = n.copy(self.part(below, 0), self.part(below, 0), n.at(y=(n.y + 1) % NY))
        self.over.append(n.copy(self.part(below, None), self.part(below, None), n.at(c=1 - n.c)))
        self.down.wait_recv()
        self.down2 = n.copy(self.part(above, 1), self.part(above, 1), n.at(y=(n.y + NY - 1) % NY))
        self.over.append(n.copy(self.part(above, None), self.part(above, None), n.at(c=1 - n.c)))

    def relay_far(self):
        n = self.net
        far = ((n.y + 2) % NY) * 2 + n.c
        self.up2.wait_recv()
        self.over.append(n.copy(self.part(far, 0), self.part(far, 0), n.at(c=1 - n.c)))
        self.down2.wait_recv()
        self.over.append(n.copy(self.part(far, 1), self.part(far, 1), n.at(c=1 - n.c)))

    def done(self):
        for made in self.over:
            made.wait_recv()


class GatherNear:
    def __init__(self, net, part):
        self.net, self.part = net, part

    def start(self):
        n = self.net
        own = self.part(n.y * 2 + n.c, None)
        self.near = [n.copy(own, own, n.at(y=(n.y + o) % NY)) for o in (1, 3, 2)]
        self.over = [n.copy(own, own, n.at(c=1 - n.c))]

    def relay(self):
        n = self.net
        for o, made in zip((1, 3, 2), self.near):
            made.wait_recv()
            slot = self.part((n.y + NY - o) % NY * 2 + n.c, None)
            self.over.append(n.copy(slot, slot, n.at(c=1 - n.c)))

    def done(self):
        for made in self.over:
            made.wait_recv()


class GatherMp:
    def __init__(self, net, block):
        self.net, self.block = net, block

    def start(self):
        n = self.net
        own = self.block.at[n.z, n.x]
        self.a = [n.copy(own, own, n.at(x=(n.x + o) % NX)) for o in range(1, NX)]
        self.s = 0

    def step(self):
        n, s = self.net, self.s
        if s == 0:
            for made in self.a:
                made.wait_recv()
        else:
            self.up.wait_recv()
            if s <= NZ // 2 - 1:
                self.down.wait_recv()
        if s < NZ // 2:
            up = self.block.at[(n.z + NZ - s) % NZ]
            self.up = n.copy(up, up, n.at(z=(n.z + 1) % NZ))
        if s < NZ // 2 - 1:
            down = self.block.at[(n.z + s) % NZ]
            self.down = n.copy(down, down, n.at(z=(n.z + NZ - 1) % NZ))
        self.s += 1


def body(x_hbm, g_hbm, w_hbm, ei_hbm, di_hbm, eo_hbm, do_hbm, post_ref, gin_ref,
         xin, g, w, ei, di, eo, do, part, got_x, row, got_z, full, edits, grads, total, cot,
         bpart, bgot_x, brow, bgot_z, zpart, zgot_z, zrow, zgot_x, send, recv, load):
    net = Links(send, recv)
    z, x, y, c = net.z, net.x, net.y, net.c
    d = y * 2 + c

    loads = []
    for k, (src, dst) in enumerate(((x_hbm, xin.at[z, x]), (ei_hbm, ei), (g_hbm, g), (eo_hbm, eo),
                                    (di_hbm, di), (do_hbm, do), (w_hbm, w.at[d]))):
        made = pltpu.make_async_copy(src, dst, load.at[k])
        made.start()
        loads.append(made)

    barrier = pltpu.get_barrier_semaphore()
    peers = ([net.at(x=(x + o) % NX) for o in range(1, NX)] + [net.at(z=(z + o) % NZ) for o in range(1, NZ)]
             + [net.at(y=(y + o) % NY) for o in range(1, NY)] + [net.at(c=1 - c)])
    for peer in peers:
        pl.semaphore_signal(barrier, inc=1, device_id=peer, device_id_type=MESH)

    def w_part(slot, half):
        return w.at[slot] if half is None else w.at[slot, pl.ds(2 * half, 2)]

    def rows_of(ref):
        def pick(slot, half):
            count = TOK if half is None else TOK // 2
            return ref.at[pl.ds(pl.multiple_of(slot * TOK + (half or 0) * count, 32), count)]
        return pick

    whole_w = GatherDp(net, w_part)
    whole_in = GatherMp(net, xin)
    loads[0].wait()
    own = xin[z, x]

    def project(value, enc, out):
        for k in range(7):
            block = nn(value, enc[:, 256 * k:256 * k + 256])
            out[:, k] = block.astype(BF16).reshape(NX, ROWS, 256)
        last = nn(value, enc[:, 1792:1920])
        out[:, 7, :, 0:128] = last.astype(BF16).reshape(NX, ROWS, 128)
        wide = value.astype(F32)
        square = wide * wide
        fold = square[:, 0:128]
        for k in range(1, value.shape[1] // 128):
            fold = fold + square[:, 128 * k:128 * k + 128]
        out[:, 7, :, 128:256] = fold.astype(BF16).reshape(NX, ROWS, 128)

    reduce_in, reduce_out, reduce_kernel, reduce_back = [
        AllReduce(net, part.at[k], got_x.at[k], row.at[k], got_z.at[k], full.at[k], 8 if k < 2 else 6)
        for k in range(4)]

    loads[1].wait()
    project(own, ei, part.at[0])
    pl.semaphore_wait(barrier, len(peers))
    reduce_in.scatter_x()
    whole_w.start(w_hbm)
    loads[2].wait()
    loads[3].wait()
    project(g[...], eo, part.at[1])
    total[...] = jnp.zeros_like(total)
    for made in loads[4:]:
        made.wait()
    reduce_in.scatter_z()
    reduce_out.scatter_x()
    whole_in.start()
    reduce_in.gather_z()
    reduce_in.gather_x()
    whole_in.step()
    reduce_out.scatter_z()

    def edit(value, hidden, dec, features):
        squares = hidden[:, 7, :, 128:256].astype(F32).reshape(TOK, 128)
        scale = lax.rsqrt(jnp.sum(squares, axis=1, keepdims=True) / features + epsilon)
        out = value.astype(F32)
        for k in range(8):
            width = 256 if k < 7 else 128
            h = hidden[:, k, :, 0:width].astype(F32).reshape(TOK, width)
            h = jnp.maximum(h * scale, 0.0).astype(BF16)
            out = out + nn(h, dec[256 * k:256 * k + width, :])
        return out.astype(BF16)

    gather_edits = GatherNear(net, rows_of(edits))
    gather_grads = GatherNear(net, rows_of(grads))
    reduce_in.done()
    rows_own = pl.ds(pl.multiple_of(d * TOK, 64), TOK)
    edits[rows_own, :] = edit(own, full.at[0], di, D)
    gather_edits.start()
    reduce_out.gather_z()
    gather_edits.relay()
    whole_in.step()
    gather_edits.done()

    def inner(k, _):
        some = edits[pl.ds(pl.multiple_of(k * 256, 256), 256), :]
        part[2, :, k] = nt(own, some).astype(BF16).reshape(NX, ROWS, 256)
        return 0
    lax.fori_loop(0, 6, inner, 0)
    reduce_kernel.scatter_x()
    whole_w.relay()
    reduce_kernel.scatter_z()
    reduce_out.gather_x()
    whole_in.step()
    reduce_kernel.gather_z()
    reduce_out.done()
    grads[rows_own, :] = edit(g[...], full.at[1], do, FW)
    gather_grads.start()
    whole_in.step()
    whole_w.relay_far()
    reduce_kernel.gather_x()
    gather_grads.relay()
    whole_in.step()
    whole_w.done()

    def base(k, _):
        value = nn(xin[k, 0], w[k, 0])
        for j in range(1, NX):
            value = value + nn(xin[k, j], w[k, j])
        total[...] += value
        return 0
    lax.fori_loop(0, NZ, base, 0)
    gather_grads.done()
    reduce_kernel.done()

    def correct(k, _):
        block = (full[2, :, k].astype(F32) * FACTOR).astype(BF16).reshape(TOK, 256)
        total[...] -= nn(block, grads[pl.ds(pl.multiple_of(k * 256, 256), 256), :])
        return 0
    lax.fori_loop(0, 6, correct, 0)

    def activate(k, _):
        rows = pl.ds(k * ROWS, ROWS)
        post = total[rows, :]
        post_ref[rows, :] = post.astype(BF16)
        sig = jax.nn.sigmoid(post)
        cot[rows, :] = (g[rows, :].astype(F32) * (sig * (1.0 + post * (1.0 - sig)))).astype(BF16)
        return 0
    lax.fori_loop(0, NX, activate, 0)

    def back_inner(k, _):
        some = grads[pl.ds(pl.multiple_of(k * 256, 256), 256), :]
        part[3, :, k] = nt(cot[...], some).astype(BF16).reshape(NX, ROWS, 256)
        return 0
    lax.fori_loop(0, 6, back_inner, 0)
    reduce_back.scatter_x()

    def back_block(k, _):
        for j in range(NX):
            value = nt(cot[...], w[k, j]).astype(BF16).reshape(NX, ROWS, 256)
            for p in range(3):
                bpart[p, j, k] = value[p]
            zpart[k, j] = value[3]
        return 0
    lax.fori_loop(0, NZ, back_block, 0)
    pieces = [AllReduce(net, bpart.at[p], bgot_x.at[p], brow.at[p], bgot_z.at[p], None) for p in range(3)]
    last = ScatterZX(net, zpart, zgot_z, zrow, zgot_x)
    pieces[0].scatter_x()
    last.scatter_z()
    reduce_back.scatter_z()
    pieces[1].scatter_x()
    pieces[2].scatter_x()
    pieces[0].scatter_z()
    reduce_back.gather_z()
    pieces[1].scatter_z()
    last.scatter_x()
    pieces[2].scatter_z()
    reduce_back.gather_x()
    reduce_back.done()
    result = jnp.zeros((TOK, 256), F32)
    for k in range(6):
        block = (full[3, :, k].astype(F32) * FACTOR).astype(BF16).reshape(TOK, 256)
        result = result - nn(block, edits[256 * k:256 * k + 256, :])
    sums = [last.sum_x()]
    sums = [piece.sum_z() for piece in pieces] + sums
    for p in range(NX):
        rows = slice(ROWS * p, ROWS * p + ROWS)
        gin_ref[rows, :] = (result[rows] + sums[p]).astype(BF16)

    net.finish()


COPIES = 176


def shards(inputs, out_grads, weight, enc_in, dec_in, enc_out, dec_out):
    anywhere = pl.BlockSpec(memory_space=pl.ANY)
    vmem = pl.BlockSpec(memory_space=pltpu.VMEM)
    scratch = [
        pltpu.VMEM((NZ, NX, TOK, 256), BF16),
        pltpu.VMEM((TOK, 512), BF16),
        pltpu.VMEM((8, 4, 256, 512), BF16),
        pltpu.VMEM((256, R), BF16),
        pltpu.VMEM((R, 256), BF16),
        pltpu.VMEM((512, R), BF16),
        pltpu.VMEM((R, 512), BF16),
        pltpu.VMEM((4, NX, NZ, ROWS, 256), BF16),
        pltpu.VMEM((4, NX - 1, NZ, ROWS, 256), BF16),
        pltpu.VMEM((4, NZ, ROWS, 256), BF16),
        pltpu.VMEM((4, NZ - 1, ROWS, 256), BF16),
        pltpu.VMEM((4, NX, NZ, ROWS, 256), BF16),
        pltpu.VMEM((8 * TOK, 256), BF16),
        pltpu.VMEM((8 * TOK, 512), BF16),
        pltpu.VMEM((TOK, 512), F32),
        pltpu.VMEM((TOK, 512), BF16),
        pltpu.VMEM((3, NX, NZ, ROWS, 256), BF16),
        pltpu.VMEM((3, NX - 1, NZ, ROWS, 256), BF16),
        pltpu.VMEM((3, NZ, ROWS, 256), BF16),
        pltpu.VMEM((3, NZ - 1, ROWS, 256), BF16),
        pltpu.VMEM((NZ, NX, ROWS, 256), BF16),
        pltpu.VMEM((NZ - 1, NX, ROWS, 256), BF16),
        pltpu.VMEM((NX, ROWS, 256), BF16),
        pltpu.VMEM((NX - 1, ROWS, 256), BF16),
        pltpu.SemaphoreType.DMA((COPIES,)),
        pltpu.SemaphoreType.DMA((COPIES,)),
        pltpu.SemaphoreType.DMA((7,)),
    ]
    return pl.pallas_call(
        body,
        out_shape=(jax.ShapeDtypeStruct((TOK, 512), BF16), jax.ShapeDtypeStruct((TOK, 256), BF16)),
        in_specs=[anywhere] * 7,
        out_specs=(vmem, vmem),
        scratch_shapes=scratch,
        compiler_params=pltpu.CompilerParams(
            collective_id=0, has_side_effects=True, vmem_limit_bytes=60 * 1024 * 1024),
    )(inputs, out_grads, weight.reshape(4, 256, 512), enc_in, dec_in, enc_out, dec_out)


def solution(mesh):
    in_specs = (
        P("dp", "mp"),
        P("dp", "mp"),
        P("dp", "mp"),
        P("mp", None),
        P(None, "mp"),
        P("mp", None),
        P(None, "mp"),
    )
    out_specs = (P("dp", "mp"), P("dp", "mp"))
    return jax.shard_map(shards, mesh=mesh, in_specs=in_specs, out_specs=out_specs, check_vma=False)
```

```python
import functools

import jax
import jax.numpy as jnp
from jax import lax
from jax.experimental import pallas as pl
from jax.experimental.pallas import tpu as pltpu
from jax.sharding import PartitionSpec as P

D = 8192
FW = 16384
R = 1920
NZ, NX, NY = 8, 4, 4
TOK = 192
ROWS = TOK // NX
epsilon = 1e-06
FACTOR = 0.25 / D
F32 = jnp.float32
BF16 = jnp.bfloat16
MESH = pl.DeviceIdType.MESH


def nn(a, b):
    return lax.dot_general(a, b, (((1,), (0,)), ((), ())), preferred_element_type=F32)


def nt(a, b):
    return lax.dot_general(a, b, (((1,), (1,)), ((), ())), preferred_element_type=F32)


def given(when, act):
    if when is None:
        act()
    else:
        pl.when(when)(act)


class Links:
    def __init__(self, send, recv):
        self.send, self.recv, self.used, self.sent = send, recv, 0, []
        mp, dp = lax.axis_index("mp"), lax.axis_index("dp")
        self.z, self.x = mp // NX, mp % NX
        self.y, self.c = dp // 2, dp % 2

    def at(self, z=None, x=None, y=None, c=None):
        z = self.z if z is None else z
        x = self.x if x is None else x
        y = self.y if y is None else y
        c = self.c if c is None else c
        return (z * NX + x, y * 2 + c)

    def copy(self, src, dst, device, when=None):
        k = self.used
        self.used += 1
        made = pltpu.make_async_remote_copy(
            src_ref=src, dst_ref=dst, send_sem=self.send.at[k], recv_sem=self.recv.at[k],
            device_id=device, device_id_type=MESH)
        given(when, made.start)
        self.sent.append((made, when))
        return made

    def finish(self):
        for made, when in self.sent:
            given(when, made.wait_send)


class AllReduce:
    def __init__(self, net, part, got_x, row, got_z, full, blocks=NZ):
        self.net, self.part, self.got_x, self.row, self.got_z, self.full = net, part, got_x, row, got_z, full
        self.blocks = blocks

    def all(self, ref, i):
        return ref.at[i] if self.blocks == NZ else ref.at[i, pl.ds(0, self.blocks)]

    def keeps(self, z):
        return None if self.blocks == NZ else z % 4 != 3

    def block(self, z):
        return z if self.blocks == NZ else z // 4 * 3 + jnp.minimum(z % 4, 2)

    def scatter_x(self):
        n = self.net
        self.a = [n.copy(self.all(self.part, (n.x + o) % NX), self.all(self.got_x, o - 1), n.at(x=(n.x + o) % NX))
                  for o in range(1, NX)]

    def scatter_z(self):
        n = self.net
        for made in self.a:
            made.wait_recv()

        def add(k, _):
            total = self.part[n.x, k].astype(F32)
            for o in range(NX - 1):
                total = total + self.got_x[o, k].astype(F32)
            self.row[k] = total.astype(BF16)
            return 0
        lax.fori_loop(0, self.blocks, add, 0)
        self.b = []
        for o in range(1, NZ):
            to = (n.z + o) % NZ
            self.b.append(n.copy(self.row.at[self.block(to)], self.got_z.at[o - 1], n.at(z=to), self.keeps(to)))

    def sum_z(self):
        for made in self.b:
            made.wait_recv()
        total = self.row[self.block(self.net.z)].astype(F32)
        for o in range(NZ - 1):
            total = total + self.got_z[o].astype(F32)
        return total

    def gather_z(self):
        n = self.net
        mine = self.block(n.z)

        def settle():
            self.full[n.x, mine] = self.sum_z().astype(BF16)
        given(self.keeps(n.z), settle)
        self.d = [n.copy(self.full.at[n.x, mine], self.full.at[n.x, mine], n.at(z=(n.z + o) % NZ), self.keeps(n.z))
                  for o in range(1, NZ)]

    def gather_x(self):
        n = self.net
        for o, made in enumerate(self.d, 1):
            given(self.keeps((n.z + NZ - o) % NZ), made.wait_recv)
        own = self.all(self.full, n.x)
        self.e = [n.copy(own, own, n.at(x=(n.x + o) % NX)) for o in range(1, NX)]

    def done(self):
        for made in self.e:
            made.wait_recv()


class ScatterZX:
    def __init__(self, net, part, got_z, row, got_x):
        self.net, self.part, self.got_z, self.row, self.got_x = net, part, got_z, row, got_x

    def scatter_z(self):
        n = self.net
        self.a = [n.copy(self.part.at[(n.z + o) % NZ], self.got_z.at[o - 1], n.at(z=(n.z + o) % NZ))
                  for o in range(1, NZ)]

    def scatter_x(self):
        n = self.net
        for made in self.a:
            made.wait_recv()

        def add(k, _):
            total = self.part[n.z, k].astype(F32)
            for o in range(NZ - 1):
                total = total + self.got_z[o, k].astype(F32)
            self.row[k] = total.astype(BF16)
            return 0
        lax.fori_loop(0, NX, add, 0)
        self.b = [n.copy(self.row.at[(n.x + o) % NX], self.got_x.at[o - 1], n.at(x=(n.x + o) % NX))
                  for o in range(1, NX)]

    def sum_x(self):
        for made in self.b:
            made.wait_recv()
        total = self.row[self.net.x].astype(F32)
        for o in range(NX - 1):
            total = total + self.got_x[o].astype(F32)
        return total


class GatherDp:
    def __init__(self, net, part):
        self.net, self.part = net, part

    def start(self, src=None):
        n = self.net
        d = n.y * 2 + n.c
        own = self.part(d, None)
        src = own if src is None else src
        self.up = n.copy(src, own, n.at(y=(n.y + 1) % NY))
        self.down = n.copy(src, own, n.at(y=(n.y + NY - 1) % NY))
        self.over = [n.copy(src, own, n.at(c=1 - n.c))]

    def relay(self):
        n = self.net
        below = ((n.y + NY - 1) % NY) * 2 + n.c
        above = ((n.y + 1) % NY) * 2 + n.c
        self.up.wait_recv()
        self.up2 = n.copy(self.part(below, 0), self.part(below, 0), n.at(y=(n.y + 1) % NY))
        self.over.append(n.copy(self.part(below, None), self.part(below, None), n.at(c=1 - n.c)))
        self.down.wait_recv()
        self.down2 = n.copy(self.part(above, 1), self.part(above, 1), n.at(y=(n.y + NY - 1) % NY))
        self.over.append(n.copy(self.part(above, None), self.part(above, None), n.at(c=1 - n.c)))

    def relay_far(self):
        n = self.net
        far = ((n.y + 2) % NY) * 2 + n.c
        self.up2.wait_recv()
        self.over.append(n.copy(self.part(far, 0), self.part(far, 0), n.at(c=1 - n.c)))
        self.down2.wait_recv()
        self.over.append(n.copy(self.part(far, 1), self.part(far, 1), n.at(c=1 - n.c)))

    def done(self):
        for made in self.over:
            made.wait_recv()


class GatherNear:
    def __init__(self, net, part):
        self.net, self.part = net, part

    def start(self):
        n = self.net
        own = self.part(n.y * 2 + n.c, None)
        self.near = [n.copy(own, own, n.at(y=(n.y + o) % NY)) for o in (1, 3, 2)]
        self.over = [n.copy(own, own, n.at(c=1 - n.c))]

    def relay(self):
        n = self.net
        for o, made in zip((1, 3, 2), self.near):
            made.wait_recv()
            slot = self.part((n.y + NY - o) % NY * 2 + n.c, None)
            self.over.append(n.copy(slot, slot, n.at(c=1 - n.c)))

    def done(self):
        for made in self.over:
            made.wait_recv()


class GatherMp:
    def __init__(self, net, block):
        self.net, self.block = net, block

    def start(self):
        n = self.net
        own = self.block.at[n.z, n.x]
        self.a = [n.copy(own, own, n.at(x=(n.x + o) % NX)) for o in range(1, NX)]
        self.s = 0

    def step(self):
        n, s = self.net, self.s
        if s == 0:
            for made in self.a:
                made.wait_recv()
        else:
            self.up.wait_recv()
            self.down.wait_recv()
        if s < NZ // 2:
            up, down = (n.z + NZ - s) % NZ, (n.z + s) % NZ
            if s < NZ // 2 - 1:
                up, down = self.block.at[up], self.block.at[down]
            else:
                half = NX // 2
                up, down = self.block.at[up, pl.ds(0, half)], self.block.at[down, pl.ds(half, half)]
            self.up = n.copy(up, up, n.at(z=(n.z + 1) % NZ))
            self.down = n.copy(down, down, n.at(z=(n.z + NZ - 1) % NZ))
        self.s += 1


def body(x_hbm, g_hbm, w_hbm, ei_hbm, di_hbm, eo_hbm, do_hbm, post_ref, gin_ref,
         xin, g, w, ei, di, eo, do, part, got_x, row, got_z, full, edits, grads, total, cot,
         bpart, bgot_x, brow, bgot_z, zpart, zgot_z, zrow, zgot_x, send, recv, load):
    net = Links(send, recv)
    z, x, y, c = net.z, net.x, net.y, net.c
    d = y * 2 + c

    loads = []
    for k, (src, dst) in enumerate(((x_hbm, xin.at[z, x]), (ei_hbm, ei), (g_hbm, g), (eo_hbm, eo),
                                    (di_hbm, di), (do_hbm, do), (w_hbm, w.at[d]))):
        made = pltpu.make_async_copy(src, dst, load.at[k])
        made.start()
        loads.append(made)

    barrier = pltpu.get_barrier_semaphore()
    peers = ([net.at(x=(x + o) % NX) for o in range(1, NX)] + [net.at(z=(z + o) % NZ) for o in range(1, NZ)]
             + [net.at(y=(y + o) % NY) for o in range(1, NY)] + [net.at(c=1 - c)])
    for peer in peers:
        pl.semaphore_signal(barrier, inc=1, device_id=peer, device_id_type=MESH)

    def w_part(slot, half):
        return w.at[slot] if half is None else w.at[slot, pl.ds(2 * half, 2)]

    def rows_of(ref):
        def pick(slot, half):
            count = TOK if half is None else TOK // 2
            return ref.at[pl.ds(pl.multiple_of(slot * TOK + (half or 0) * count, 32), count)]
        return pick

    whole_w = GatherDp(net, w_part)
    whole_in = GatherMp(net, xin)
    loads[0].wait()
    own = xin[z, x]

    def project(value, enc, out):
        for k in range(7):
            block = nn(value, enc[:, 256 * k:256 * k + 256])
            out[:, k] = block.astype(BF16).reshape(NX, ROWS, 256)
        last = nn(value, enc[:, 1792:1920])
        out[:, 7, :, 0:128] = last.astype(BF16).reshape(NX, ROWS, 128)
        wide = value.astype(F32)
        square = wide * wide
        fold = square[:, 0:128]
        for k in range(1, value.shape[1] // 128):
            fold = fold + square[:, 128 * k:128 * k + 128]
        out[:, 7, :, 128:256] = fold.astype(BF16).reshape(NX, ROWS, 128)

    reduce_in, reduce_out, reduce_kernel, reduce_back = [
        AllReduce(net, part.at[k], got_x.at[k], row.at[k], got_z.at[k], full.at[k], 8 if k < 2 else 6)
        for k in range(4)]

    loads[1].wait()
    project(own, ei, part.at[0])
    pl.semaphore_wait(barrier, len(peers))
    reduce_in.scatter_x()
    whole_w.start(w_hbm)
    loads[2].wait()
    loads[3].wait()
    project(g[...], eo, part.at[1])
    total[...] = jnp.zeros_like(total)
    for made in loads[4:]:
        made.wait()
    reduce_in.scatter_z()
    reduce_out.scatter_x()
    whole_in.start()
    reduce_in.gather_z()
    reduce_in.gather_x()
    whole_in.step()
    reduce_out.scatter_z()

    def edit(value, hidden, dec, features):
        squares = hidden[:, 7, :, 128:256].astype(F32).reshape(TOK, 128)
        scale = lax.rsqrt(jnp.sum(squares, axis=1, keepdims=True) / features + epsilon)
        out = value.astype(F32)
        for k in range(8):
            width = 256 if k < 7 else 128
            h = hidden[:, k, :, 0:width].astype(F32).reshape(TOK, width)
            h = jnp.maximum(h * scale, 0.0).astype(BF16)
            out = out + nn(h, dec[256 * k:256 * k + width, :])
        return out.astype(BF16)

    gather_edits = GatherNear(net, rows_of(edits))
    gather_grads = GatherNear(net, rows_of(grads))
    reduce_in.done()
    rows_own = pl.ds(pl.multiple_of(d * TOK, 64), TOK)
    edits[rows_own, :] = edit(own, full.at[0], di, D)
    gather_edits.start()
    reduce_out.gather_z()
    gather_edits.relay()
    whole_in.step()
    gather_edits.done()

    def inner(k, _):
        some = edits[pl.ds(pl.multiple_of(k * 256, 256), 256), :]
        part[2, :, k] = nt(own, some).astype(BF16).reshape(NX, ROWS, 256)
        return 0
    lax.fori_loop(0, 6, inner, 0)
    reduce_kernel.scatter_x()
    whole_w.relay()
    reduce_kernel.scatter_z()
    reduce_out.gather_x()
    whole_in.step()
    reduce_kernel.gather_z()
    reduce_out.done()
    grads[rows_own, :] = edit(g[...], full.at[1], do, FW)
    gather_grads.start()
    whole_in.step()
    whole_w.relay_far()
    reduce_kernel.gather_x()
    gather_grads.relay()
    whole_in.step()
    whole_w.done()

    def base(k, _):
        value = nn(xin[k, 0], w[k, 0])
        for j in range(1, NX):
            value = value + nn(xin[k, j], w[k, j])
        total[...] += value
        return 0
    lax.fori_loop(0, NZ, base, 0)
    gather_grads.done()
    reduce_kernel.done()

    def correct(k, _):
        block = (full[2, :, k].astype(F32) * FACTOR).astype(BF16).reshape(TOK, 256)
        total[...] -= nn(block, grads[pl.ds(pl.multiple_of(k * 256, 256), 256), :])
        return 0
    lax.fori_loop(0, 6, correct, 0)

    def activate(k, _):
        rows = pl.ds(k * ROWS, ROWS)
        post = total[rows, :]
        post_ref[rows, :] = post.astype(BF16)
        sig = jax.nn.sigmoid(post)
        cot[rows, :] = (g[rows, :].astype(F32) * (sig * (1.0 + post * (1.0 - sig)))).astype(BF16)
        return 0
    lax.fori_loop(0, NX, activate, 0)

    def back_inner(k, _):
        some = grads[pl.ds(pl.multiple_of(k * 256, 256), 256), :]
        part[3, :, k] = nt(cot[...], some).astype(BF16).reshape(NX, ROWS, 256)
        return 0
    lax.fori_loop(0, 6, back_inner, 0)
    reduce_back.scatter_x()

    def back_block(k, _):
        for j in range(NX):
            value = nt(cot[...], w[k, j]).astype(BF16).reshape(NX, ROWS, 256)
            for p in range(3):
                bpart[p, j, k] = value[p]
            zpart[k, j] = value[3]
        return 0
    lax.fori_loop(0, NZ, back_block, 0)
    pieces = [AllReduce(net, bpart.at[p], bgot_x.at[p], brow.at[p], bgot_z.at[p], None) for p in range(3)]
    last = ScatterZX(net, zpart, zgot_z, zrow, zgot_x)
    pieces[0].scatter_x()
    last.scatter_z()
    reduce_back.scatter_z()
    pieces[1].scatter_x()
    pieces[2].scatter_x()
    pieces[0].scatter_z()
    reduce_back.gather_z()
    pieces[1].scatter_z()
    last.scatter_x()
    pieces[2].scatter_z()
    reduce_back.gather_x()
    reduce_back.done()
    result = jnp.zeros((TOK, 256), F32)
    for k in range(6):
        block = (full[3, :, k].astype(F32) * FACTOR).astype(BF16).reshape(TOK, 256)
        result = result - nn(block, edits[256 * k:256 * k + 256, :])
    sums = [last.sum_x()]
    sums = [piece.sum_z() for piece in pieces] + sums
    for p in range(NX):
        rows = slice(ROWS * p, ROWS * p + ROWS)
        gin_ref[rows, :] = (result[rows] + sums[p]).astype(BF16)

    net.finish()


COPIES = 176


def shards(inputs, out_grads, weight, enc_in, dec_in, enc_out, dec_out):
    anywhere = pl.BlockSpec(memory_space=pl.ANY)
    vmem = pl.BlockSpec(memory_space=pltpu.VMEM)
    scratch = [
        pltpu.VMEM((NZ, NX, TOK, 256), BF16),
        pltpu.VMEM((TOK, 512), BF16),
        pltpu.VMEM((8, 4, 256, 512), BF16),
        pltpu.VMEM((256, R), BF16),
        pltpu.VMEM((R, 256), BF16),
        pltpu.VMEM((512, R), BF16),
        pltpu.VMEM((R, 512), BF16),
        pltpu.VMEM((4, NX, NZ, ROWS, 256), BF16),
        pltpu.VMEM((4, NX - 1, NZ, ROWS, 256), BF16),
        pltpu.VMEM((4, NZ, ROWS, 256), BF16),
        pltpu.VMEM((4, NZ - 1, ROWS, 256), BF16),
        pltpu.VMEM((4, NX, NZ, ROWS, 256), BF16),
        pltpu.VMEM((8 * TOK, 256), BF16),
        pltpu.VMEM((8 * TOK, 512), BF16),
        pltpu.VMEM((TOK, 512), F32),
        pltpu.VMEM((TOK, 512), BF16),
        pltpu.VMEM((3, NX, NZ, ROWS, 256), BF16),
        pltpu.VMEM((3, NX - 1, NZ, ROWS, 256), BF16),
        pltpu.VMEM((3, NZ, ROWS, 256), BF16),
        pltpu.VMEM((3, NZ - 1, ROWS, 256), BF16),
        pltpu.VMEM((NZ, NX, ROWS, 256), BF16),
        pltpu.VMEM((NZ - 1, NX, ROWS, 256), BF16),
        pltpu.VMEM((NX, ROWS, 256), BF16),
        pltpu.VMEM((NX - 1, ROWS, 256), BF16),
        pltpu.SemaphoreType.DMA((COPIES,)),
        pltpu.SemaphoreType.DMA((COPIES,)),
        pltpu.SemaphoreType.DMA((7,)),
    ]
    return pl.pallas_call(
        body,
        out_shape=(jax.ShapeDtypeStruct((TOK, 512), BF16), jax.ShapeDtypeStruct((TOK, 256), BF16)),
        in_specs=[anywhere] * 7,
        out_specs=(vmem, vmem),
        scratch_shapes=scratch,
        compiler_params=pltpu.CompilerParams(
            collective_id=0, has_side_effects=True, vmem_limit_bytes=60 * 1024 * 1024),
    )(inputs, out_grads, weight.reshape(4, 256, 512), enc_in, dec_in, enc_out, dec_out)


def solution(mesh):
    in_specs = (
        P("dp", "mp"),
        P("dp", "mp"),
        P("dp", "mp"),
        P("mp", None),
        P(None, "mp"),
        P("mp", None),
        P(None, "mp"),
    )
    out_specs = (P("dp", "mp"), P("dp", "mp"))
    return jax.shard_map(shards, mesh=mesh, in_specs=in_specs, out_specs=out_specs, check_vma=False)
```

```python
import functools

import jax
import jax.numpy as jnp
from jax import lax
from jax.experimental import pallas as pl
from jax.experimental.pallas import tpu as pltpu
from jax.sharding import PartitionSpec as P

D = 8192
FW = 16384
R = 1920
NZ, NX, NY = 8, 4, 4
TOK = 192
ROWS = TOK // NX
epsilon = 1e-06
FACTOR = 0.25 / D
F32 = jnp.float32
BF16 = jnp.bfloat16
MESH = pl.DeviceIdType.MESH


def nn(a, b):
    return lax.dot_general(a, b, (((1,), (0,)), ((), ())), preferred_element_type=F32)


def nt(a, b):
    return lax.dot_general(a, b, (((1,), (1,)), ((), ())), preferred_element_type=F32)


def given(when, act):
    if when is None:
        act()
    else:
        pl.when(when)(act)


class Links:
    def __init__(self, send, recv):
        self.send, self.recv, self.used, self.sent = send, recv, 0, []
        mp, dp = lax.axis_index("mp"), lax.axis_index("dp")
        self.z, self.x = mp // NX, mp % NX
        self.y, self.c = dp // 2, dp % 2

    def at(self, z=None, x=None, y=None, c=None):
        z = self.z if z is None else z
        x = self.x if x is None else x
        y = self.y if y is None else y
        c = self.c if c is None else c
        return (z * NX + x, y * 2 + c)

    def copy(self, src, dst, device, when=None):
        k = self.used
        self.used += 1
        made = pltpu.make_async_remote_copy(
            src_ref=src, dst_ref=dst, send_sem=self.send.at[k], recv_sem=self.recv.at[k],
            device_id=device, device_id_type=MESH)
        given(when, made.start)
        self.sent.append((made, when))
        return made

    def finish(self):
        for made, when in self.sent:
            given(when, made.wait_send)


class AllReduce:
    def __init__(self, net, part, got_x, row, got_z, full, blocks=NZ):
        self.net, self.part, self.got_x, self.row, self.got_z, self.full = net, part, got_x, row, got_z, full
        self.blocks = blocks

    def all(self, ref, i):
        return ref.at[i] if self.blocks == NZ else ref.at[i, pl.ds(0, self.blocks)]

    def keeps(self, z):
        return None if self.blocks == NZ else z % 4 != 3

    def block(self, z):
        return z if self.blocks == NZ else z // 4 * 3 + jnp.minimum(z % 4, 2)

    def scatter_x(self):
        n = self.net
        self.a = [n.copy(self.all(self.part, (n.x + o) % NX), self.all(self.got_x, o - 1), n.at(x=(n.x + o) % NX))
                  for o in range(1, NX)]

    def scatter_z(self):
        n = self.net
        for made in self.a:
            made.wait_recv()

        def add(k, _):
            total = self.part[n.x, k].astype(F32)
            for o in range(NX - 1):
                total = total + self.got_x[o, k].astype(F32)
            self.row[k] = total.astype(BF16)
            return 0
        lax.fori_loop(0, self.blocks, add, 0)
        self.b = []
        for o in range(1, NZ):
            to = (n.z + o) % NZ
            self.b.append(n.copy(self.row.at[self.block(to)], self.got_z.at[o - 1], n.at(z=to), self.keeps(to)))

    def sum_z(self):
        for made in self.b:
            made.wait_recv()
        total = self.row[self.block(self.net.z)].astype(F32)
        for o in range(NZ - 1):
            total = total + self.got_z[o].astype(F32)
        return total

    def gather_z(self):
        n = self.net
        mine = self.block(n.z)

        def settle():
            self.full[n.x, mine] = self.sum_z().astype(BF16)
        given(self.keeps(n.z), settle)
        self.d = [n.copy(self.full.at[n.x, mine], self.full.at[n.x, mine], n.at(z=(n.z + o) % NZ), self.keeps(n.z))
                  for o in range(1, NZ)]

    def gather_x(self):
        n = self.net
        for o, made in enumerate(self.d, 1):
            given(self.keeps((n.z + NZ - o) % NZ), made.wait_recv)
        own = self.all(self.full, n.x)
        self.e = [n.copy(own, own, n.at(x=(n.x + o) % NX)) for o in range(1, NX)]

    def done(self):
        for made in self.e:
            made.wait_recv()


class ScatterZX:
    def __init__(self, net, part, got_z, row, got_x):
        self.net, self.part, self.got_z, self.row, self.got_x = net, part, got_z, row, got_x

    def scatter_z(self):
        n = self.net
        self.a = [n.copy(self.part.at[(n.z + o) % NZ], self.got_z.at[o - 1], n.at(z=(n.z + o) % NZ))
                  for o in range(1, NZ)]

    def scatter_x(self):
        n = self.net
        for made in self.a:
            made.wait_recv()

        def add(k, _):
            total = self.part[n.z, k].astype(F32)
            for o in range(NZ - 1):
                total = total + self.got_z[o, k].astype(F32)
            self.row[k] = total.astype(BF16)
            return 0
        lax.fori_loop(0, NX, add, 0)
        self.b = [n.copy(self.row.at[(n.x + o) % NX], self.got_x.at[o - 1], n.at(x=(n.x + o) % NX))
                  for o in range(1, NX)]

    def sum_x(self):
        for made in self.b:
            made.wait_recv()
        total = self.row[self.net.x].astype(F32)
        for o in range(NX - 1):
            total = total + self.got_x[o].astype(F32)
        return total


class GatherDp:
    def __init__(self, net, part):
        self.net, self.part = net, part

    def start(self, src=None):
        n = self.net
        d = n.y * 2 + n.c
        own = self.part(d, None)
        src = own if src is None else src
        self.up = n.copy(src, own, n.at(y=(n.y + 1) % NY))
        self.down = n.copy(src, own, n.at(y=(n.y + NY - 1) % NY))
        self.over = [n.copy(src, own, n.at(c=1 - n.c))]

    def relay(self):
        n = self.net
        below = ((n.y + NY - 1) % NY) * 2 + n.c
        above = ((n.y + 1) % NY) * 2 + n.c
        self.up.wait_recv()
        self.up2 = n.copy(self.part(below, 0), self.part(below, 0), n.at(y=(n.y + 1) % NY))
        self.over.append(n.copy(self.part(below, None), self.part(below, None), n.at(c=1 - n.c)))
        self.down.wait_recv()
        self.down2 = n.copy(self.part(above, 1), self.part(above, 1), n.at(y=(n.y + NY - 1) % NY))
        self.over.append(n.copy(self.part(above, None), self.part(above, None), n.at(c=1 - n.c)))

    def relay_far(self):
        n = self.net
        far = ((n.y + 2) % NY) * 2 + n.c
        self.up2.wait_recv()
        self.over.append(n.copy(self.part(far, 0), self.part(far, 0), n.at(c=1 - n.c)))
        self.down2.wait_recv()
        self.over.append(n.copy(self.part(far, 1), self.part(far, 1), n.at(c=1 - n.c)))

    def done(self):
        for made in self.over:
            made.wait_recv()


class GatherNear:
    def __init__(self, net, part):
        self.net, self.part = net, part

    def start(self):
        n = self.net
        own = self.part(n.y * 2 + n.c, None)
        self.near = [n.copy(own, own, n.at(y=(n.y + o) % NY)) for o in (1, 3, 2)]
        self.over = [n.copy(own, own, n.at(c=1 - n.c))]

    def relay(self):
        n = self.net
        for o, made in zip((1, 3, 2), self.near):
            made.wait_recv()
            slot = self.part((n.y + NY - o) % NY * 2 + n.c, None)
            self.over.append(n.copy(slot, slot, n.at(c=1 - n.c)))

    def done(self):
        for made in self.over:
            made.wait_recv()


class GatherMp:
    def __init__(self, net, block):
        self.net, self.block = net, block

    def start(self):
        n = self.net
        own = self.block.at[n.z, n.x]
        self.a = [n.copy(own, own, n.at(x=(n.x + o) % NX)) for o in range(1, NX)]
        self.s = 0

    def step(self):
        n, s = self.net, self.s
        if s == 0:
            for made in self.a:
                made.wait_recv()
        else:
            self.up.wait_recv()
            self.down.wait_recv()
        if s < NZ // 2:
            up, down = (n.z + NZ - s) % NZ, (n.z + s) % NZ
            if s < NZ // 2 - 1:
                up, down = self.block.at[up], self.block.at[down]
            else:
                half = NX // 2
                up, down = self.block.at[up, pl.ds(0, half)], self.block.at[down, pl.ds(half, half)]
            self.up = n.copy(up, up, n.at(z=(n.z + 1) % NZ))
            self.down = n.copy(down, down, n.at(z=(n.z + NZ - 1) % NZ))
        self.s += 1


def body(x_hbm, g_hbm, w_hbm, ei_hbm, di_hbm, eo_hbm, do_hbm, post_ref, gin_ref,
         xin, g, w, ei, di, eo, do, part, got_x, row, got_z, full, edits, grads, total, cot,
         bpart, bgot_x, brow, bgot_z, zpart, zgot_z, zrow, zgot_x, send, recv, load):
    net = Links(send, recv)
    z, x, y, c = net.z, net.x, net.y, net.c
    d = y * 2 + c

    loads = []
    for k, (src, dst) in enumerate(((x_hbm, xin.at[z, x]), (ei_hbm, ei), (g_hbm, g), (eo_hbm, eo),
                                    (di_hbm, di), (do_hbm, do), (w_hbm, w.at[d]))):
        made = pltpu.make_async_copy(src, dst, load.at[k])
        made.start()
        loads.append(made)

    barrier = pltpu.get_barrier_semaphore()
    peers = ([net.at(x=(x + o) % NX) for o in range(1, NX)] + [net.at(z=(z + o) % NZ) for o in range(1, NZ)]
             + [net.at(y=(y + o) % NY) for o in range(1, NY)] + [net.at(c=1 - c)])
    for peer in peers:
        pl.semaphore_signal(barrier, inc=1, device_id=peer, device_id_type=MESH)

    def w_part(slot, half):
        return w.at[slot] if half is None else w.at[slot, pl.ds(2 * half, 2)]

    def rows_of(ref):
        def pick(slot, half):
            count = TOK if half is None else TOK // 2
            return ref.at[pl.ds(pl.multiple_of(slot * TOK + (half or 0) * count, 32), count)]
        return pick

    whole_w = GatherDp(net, w_part)
    whole_in = GatherMp(net, xin)
    loads[0].wait()
    own = xin[z, x]

    def project(value, enc, out):
        for k in range(7):
            block = nn(value, enc[:, 256 * k:256 * k + 256])
            out[:, k] = block.astype(BF16).reshape(NX, ROWS, 256)
        last = nn(value, enc[:, 1792:1920])
        out[:, 7, :, 0:128] = last.astype(BF16).reshape(NX, ROWS, 128)
        wide = value.astype(F32)
        square = wide * wide
        fold = square[:, 0:128]
        for k in range(1, value.shape[1] // 128):
            fold = fold + square[:, 128 * k:128 * k + 128]
        out[:, 7, :, 128:256] = fold.astype(BF16).reshape(NX, ROWS, 128)

    reduce_in, reduce_out, reduce_kernel, reduce_back = [
        AllReduce(net, part.at[k], got_x.at[k], row.at[k], got_z.at[k], full.at[k], 8 if k < 2 else 6)
        for k in range(4)]

    loads[1].wait()
    project(own, ei, part.at[0])
    pl.semaphore_wait(barrier, len(peers))
    reduce_in.scatter_x()
    whole_w.start(w_hbm)
    loads[2].wait()
    loads[3].wait()
    project(g[...], eo, part.at[1])
    total[...] = jnp.zeros_like(total)
    for made in loads[4:]:
        made.wait()
    reduce_in.scatter_z()
    reduce_out.scatter_x()
    whole_in.start()
    reduce_in.gather_z()
    reduce_in.gather_x()
    whole_in.step()
    reduce_out.scatter_z()

    def edit(value, hidden, dec, features):
        squares = hidden[:, 7, :, 128:256].astype(F32).reshape(TOK, 128)
        scale = lax.rsqrt(jnp.sum(squares, axis=1, keepdims=True) / features + epsilon)
        out = value.astype(F32)
        for k in range(8):
            width = 256 if k < 7 else 128
            h = hidden[:, k, :, 0:width].astype(F32).reshape(TOK, width)
            h = jnp.maximum(h * scale, 0.0).astype(BF16)
            out = out + nn(h, dec[256 * k:256 * k + width, :])
        return out.astype(BF16)

    gather_edits = GatherNear(net, rows_of(edits))
    gather_grads = GatherNear(net, rows_of(grads))
    reduce_in.done()
    rows_own = pl.ds(pl.multiple_of(d * TOK, 64), TOK)
    edits[rows_own, :] = edit(own, full.at[0], di, D)
    gather_edits.start()
    reduce_out.gather_z()
    gather_edits.relay()
    whole_in.step()
    gather_edits.done()

    def inner(k, _):
        some = edits[pl.ds(pl.multiple_of(k * 256, 256), 256), :]
        part[2, :, k] = nt(own, some).astype(BF16).reshape(NX, ROWS, 256)
        return 0
    lax.fori_loop(0, 6, inner, 0)
    reduce_kernel.scatter_x()
    whole_w.relay()
    reduce_kernel.scatter_z()
    reduce_out.gather_x()
    whole_in.step()
    reduce_kernel.gather_z()
    whole_in.step()
    reduce_out.done()
    grads[rows_own, :] = edit(g[...], full.at[1], do, FW)
    gather_grads.start()
    whole_w.relay_far()
    reduce_kernel.gather_x()
    gather_grads.relay()
    whole_in.step()
    whole_w.done()

    def base(k, _):
        value = nn(xin[k, 0], w[k, 0])
        for j in range(1, NX):
            value = value + nn(xin[k, j], w[k, j])
        total[...] += value
        return 0
    lax.fori_loop(0, NZ, base, 0)
    gather_grads.done()
    reduce_kernel.done()

    def correct(k, _):
        block = (full[2, :, k].astype(F32) * FACTOR).astype(BF16).reshape(TOK, 256)
        total[...] -= nn(block, grads[pl.ds(pl.multiple_of(k * 256, 256), 256), :])
        return 0
    lax.fori_loop(0, 6, correct, 0)

    def activate(k, _):
        rows = pl.ds(k * ROWS, ROWS)
        post = total[rows, :]
        post_ref[rows, :] = post.astype(BF16)
        sig = jax.nn.sigmoid(post)
        cot[rows, :] = (g[rows, :].astype(F32) * (sig * (1.0 + post * (1.0 - sig)))).astype(BF16)
        return 0
    lax.fori_loop(0, NX, activate, 0)

    def back_inner(k, _):
        some = grads[pl.ds(pl.multiple_of(k * 256, 256), 256), :]
        part[3, :, k] = nt(cot[...], some).astype(BF16).reshape(NX, ROWS, 256)
        return 0
    lax.fori_loop(0, 6, back_inner, 0)
    reduce_back.scatter_x()

    def back_block(k, _):
        for j in range(NX):
            value = nt(cot[...], w[k, j]).astype(BF16).reshape(NX, ROWS, 256)
            for p in range(3):
                bpart[p, j, k] = value[p]
            zpart[k, j] = value[3]
        return 0
    lax.fori_loop(0, NZ, back_block, 0)
    pieces = [AllReduce(net, bpart.at[p], bgot_x.at[p], brow.at[p], bgot_z.at[p], None) for p in range(3)]
    last = ScatterZX(net, zpart, zgot_z, zrow, zgot_x)
    pieces[0].scatter_x()
    last.scatter_z()
    reduce_back.scatter_z()
    pieces[1].scatter_x()
    pieces[2].scatter_x()
    pieces[0].scatter_z()
    reduce_back.gather_z()
    pieces[1].scatter_z()
    last.scatter_x()
    pieces[2].scatter_z()
    reduce_back.gather_x()
    reduce_back.done()
    result = jnp.zeros((TOK, 256), F32)
    for k in range(6):
        block = (full[3, :, k].astype(F32) * FACTOR).astype(BF16).reshape(TOK, 256)
        result = result - nn(block, edits[256 * k:256 * k + 256, :])
    sums = [last.sum_x()]
    sums = [piece.sum_z() for piece in pieces] + sums
    for p in range(NX):
        rows = slice(ROWS * p, ROWS * p + ROWS)
        gin_ref[rows, :] = (result[rows] + sums[p]).astype(BF16)

    net.finish()


COPIES = 176


def shards(inputs, out_grads, weight, enc_in, dec_in, enc_out, dec_out):
    anywhere = pl.BlockSpec(memory_space=pl.ANY)
    vmem = pl.BlockSpec(memory_space=pltpu.VMEM)
    scratch = [
        pltpu.VMEM((NZ, NX, TOK, 256), BF16),
        pltpu.VMEM((TOK, 512), BF16),
        pltpu.VMEM((8, 4, 256, 512), BF16),
        pltpu.VMEM((256, R), BF16),
        pltpu.VMEM((R, 256), BF16),
        pltpu.VMEM((512, R), BF16),
        pltpu.VMEM((R, 512), BF16),
        pltpu.VMEM((4, NX, NZ, ROWS, 256), BF16),
        pltpu.VMEM((4, NX - 1, NZ, ROWS, 256), BF16),
        pltpu.VMEM((4, NZ, ROWS, 256), BF16),
        pltpu.VMEM((4, NZ - 1, ROWS, 256), BF16),
        pltpu.VMEM((4, NX, NZ, ROWS, 256), BF16),
        pltpu.VMEM((8 * TOK, 256), BF16),
        pltpu.VMEM((8 * TOK, 512), BF16),
        pltpu.VMEM((TOK, 512), F32),
        pltpu.VMEM((TOK, 512), BF16),
        pltpu.VMEM((3, NX, NZ, ROWS, 256), BF16),
        pltpu.VMEM((3, NX - 1, NZ, ROWS, 256), BF16),
        pltpu.VMEM((3, NZ, ROWS, 256), BF16),
        pltpu.VMEM((3, NZ - 1, ROWS, 256), BF16),
        pltpu.VMEM((NZ, NX, ROWS, 256), BF16),
        pltpu.VMEM((NZ - 1, NX, ROWS, 256), BF16),
        pltpu.VMEM((NX, ROWS, 256), BF16),
        pltpu.VMEM((NX - 1, ROWS, 256), BF16),
        pltpu.SemaphoreType.DMA((COPIES,)),
        pltpu.SemaphoreType.DMA((COPIES,)),
        pltpu.SemaphoreType.DMA((7,)),
    ]
    return pl.pallas_call(
        body,
        out_shape=(jax.ShapeDtypeStruct((TOK, 512), BF16), jax.ShapeDtypeStruct((TOK, 256), BF16)),
        in_specs=[anywhere] * 7,
        out_specs=(vmem, vmem),
        scratch_shapes=scratch,
        compiler_params=pltpu.CompilerParams(
            collective_id=0, has_side_effects=True, vmem_limit_bytes=60 * 1024 * 1024),
    )(inputs, out_grads, weight.reshape(4, 256, 512), enc_in, dec_in, enc_out, dec_out)


def solution(mesh):
    in_specs = (
        P("dp", "mp"),
        P("dp", "mp"),
        P("dp", "mp"),
        P("mp", None),
        P(None, "mp"),
        P("mp", None),
        P(None, "mp"),
    )
    out_specs = (P("dp", "mp"), P("dp", "mp"))
    return jax.shard_map(shards, mesh=mesh, in_specs=in_specs, out_specs=out_specs, check_vma=False)
```

```python
import functools

import jax
import jax.numpy as jnp
from jax import lax
from jax.experimental import pallas as pl
from jax.experimental.pallas import tpu as pltpu
from jax.sharding import PartitionSpec as P

D = 8192
FW = 16384
R = 1920
NZ, NX, NY = 8, 4, 4
TOK = 192
ROWS = TOK // NX
epsilon = 1e-06
FACTOR = 0.25 / D
F32 = jnp.float32
BF16 = jnp.bfloat16
MESH = pl.DeviceIdType.MESH


def nn(a, b):
    return lax.dot_general(a, b, (((1,), (0,)), ((), ())), preferred_element_type=F32)


def nt(a, b):
    return lax.dot_general(a, b, (((1,), (1,)), ((), ())), preferred_element_type=F32)


def given(when, act):
    if when is None:
        act()
    else:
        pl.when(when)(act)


class Links:
    def __init__(self, send, recv):
        self.send, self.recv, self.used, self.sent = send, recv, 0, []
        mp, dp = lax.axis_index("mp"), lax.axis_index("dp")
        self.z, self.x = mp // NX, mp % NX
        self.y, self.c = dp // 2, dp % 2

    def at(self, z=None, x=None, y=None, c=None):
        z = self.z if z is None else z
        x = self.x if x is None else x
        y = self.y if y is None else y
        c = self.c if c is None else c
        return (z * NX + x, y * 2 + c)

    def copy(self, src, dst, device, when=None):
        k = self.used
        self.used += 1
        made = pltpu.make_async_remote_copy(
            src_ref=src, dst_ref=dst, send_sem=self.send.at[k], recv_sem=self.recv.at[k],
            device_id=device, device_id_type=MESH)
        given(when, made.start)
        self.sent.append((made, when))
        return made

    def finish(self):
        for made, when in self.sent:
            given(when, made.wait_send)


class AllReduce:
    arrivals = NX - 1

    def __init__(self, net, part, got_x, row, got_z, full, blocks=NZ):
        self.net, self.part, self.got_x, self.row, self.got_z, self.full = net, part, got_x, row, got_z, full
        self.blocks = blocks

    def all(self, ref, i):
        return ref.at[i] if self.blocks == NZ else ref.at[i, pl.ds(0, self.blocks)]

    def keeps(self, z):
        return None if self.blocks == NZ else z % 4 != 3

    def block(self, z):
        return z if self.blocks == NZ else z // 4 * 3 + jnp.minimum(z % 4, 2)

    def scatter_x(self):
        n = self.net
        self.a = [n.copy(self.all(self.part, (n.x + o) % NX), self.all(self.got_x, o - 1), n.at(x=(n.x + o) % NX))
                  for o in range(1, NX)]

    def scatter_z(self):
        n = self.net
        for made in self.a:
            made.wait_recv()

        def add(k, _):
            total = self.part[n.x, k].astype(F32)
            for o in range(self.arrivals):
                total = total + self.got_x[o, k].astype(F32)
            self.row[k] = total.astype(BF16)
            return 0
        lax.fori_loop(0, self.blocks, add, 0)
        self.b = []
        for o in range(1, NZ):
            to = (n.z + o) % NZ
            self.b.append(n.copy(self.row.at[self.block(to)], self.got_z.at[o - 1], n.at(z=to), self.keeps(to)))

    def sum_z(self):
        for made in self.b:
            made.wait_recv()
        total = self.row[self.block(self.net.z)].astype(F32)
        for o in range(NZ - 1):
            total = total + self.got_z[o].astype(F32)
        return total

    def gather_z(self):
        n = self.net
        mine = self.block(n.z)

        def settle():
            self.full[n.x, mine] = self.sum_z().astype(BF16)
        given(self.keeps(n.z), settle)
        self.d = [n.copy(self.full.at[n.x, mine], self.full.at[n.x, mine], n.at(z=(n.z + o) % NZ), self.keeps(n.z))
                  for o in range(1, NZ)]

    def gather_x(self):
        n = self.net
        for o, made in enumerate(self.d, 1):
            given(self.keeps((n.z + NZ - o) % NZ), made.wait_recv)
        own = self.all(self.full, n.x)
        self.e = [n.copy(own, own, n.at(x=(n.x + o) % NX)) for o in range(1, NX)]

    def done(self):
        for made in self.e:
            made.wait_recv()


class RelayedScatter(AllReduce):
    arrivals = 2

    def scatter_x(self):
        n, half = self.net, NZ // 2
        far = (n.x + 2) % NX
        low, high = pl.ds(0, half), pl.ds(half, half)
        self.far_up = n.copy(self.part.at[far, low], self.got_x.at[2, low], n.at(x=(n.x + 1) % NX))
        self.far_down = n.copy(self.part.at[far, high], self.got_x.at[2, high], n.at(x=(n.x + 3) % NX))

    def relay_x(self):
        n, half = self.net, NZ // 2
        up, down = (n.x + 1) % NX, (n.x + 3) % NX
        self.far_up.wait_recv()
        self.far_down.wait_recv()

        def add(k, _):
            self.part[up, k] = (self.part[up, k].astype(F32) + self.got_x[2, k].astype(F32)).astype(BF16)
            h = k + half
            self.part[down, h] = (self.part[down, h].astype(F32) + self.got_x[2, h].astype(F32)).astype(BF16)
            return 0
        lax.fori_loop(0, half, add, 0)
        self.a = [n.copy(self.part.at[up], self.got_x.at[0], n.at(x=up)),
                  n.copy(self.part.at[down], self.got_x.at[1], n.at(x=down))]


class ScatterZX:
    def __init__(self, net, part, got_z, row, got_x):
        self.net, self.part, self.got_z, self.row, self.got_x = net, part, got_z, row, got_x

    def scatter_z(self):
        n = self.net
        self.a = [n.copy(self.part.at[(n.z + o) % NZ], self.got_z.at[o - 1], n.at(z=(n.z + o) % NZ))
                  for o in range(1, NZ)]

    def scatter_x(self):
        n = self.net
        for made in self.a:
            made.wait_recv()

        def add(k, _):
            total = self.part[n.z, k].astype(F32)
            for o in range(NZ - 1):
                total = total + self.got_z[o, k].astype(F32)
            self.row[k] = total.astype(BF16)
            return 0
        lax.fori_loop(0, NX, add, 0)
        self.b = [n.copy(self.row.at[(n.x + o) % NX], self.got_x.at[o - 1], n.at(x=(n.x + o) % NX))
                  for o in range(1, NX)]

    def sum_x(self):
        for made in self.b:
            made.wait_recv()
        total = self.row[self.net.x].astype(F32)
        for o in range(NX - 1):
            total = total + self.got_x[o].astype(F32)
        return total


class GatherDp:
    def __init__(self, net, part):
        self.net, self.part = net, part

    def start(self, src=None):
        n = self.net
        d = n.y * 2 + n.c
        own = self.part(d, None)
        src = own if src is None else src
        self.up = n.copy(src, own, n.at(y=(n.y + 1) % NY))
        self.down = n.copy(src, own, n.at(y=(n.y + NY - 1) % NY))
        self.over = [n.copy(src, own, n.at(c=1 - n.c))]

    def relay(self):
        n = self.net
        below = ((n.y + NY - 1) % NY) * 2 + n.c
        above = ((n.y + 1) % NY) * 2 + n.c
        self.up.wait_recv()
        self.up2 = n.copy(self.part(below, 0), self.part(below, 0), n.at(y=(n.y + 1) % NY))
        self.over.append(n.copy(self.part(below, None), self.part(below, None), n.at(c=1 - n.c)))
        self.down.wait_recv()
        self.down2 = n.copy(self.part(above, 1), self.part(above, 1), n.at(y=(n.y + NY - 1) % NY))
        self.over.append(n.copy(self.part(above, None), self.part(above, None), n.at(c=1 - n.c)))

    def relay_far(self):
        n = self.net
        far = ((n.y + 2) % NY) * 2 + n.c
        self.up2.wait_recv()
        self.over.append(n.copy(self.part(far, 0), self.part(far, 0), n.at(c=1 - n.c)))
        self.down2.wait_recv()
        self.over.append(n.copy(self.part(far, 1), self.part(far, 1), n.at(c=1 - n.c)))

    def done(self):
        for made in self.over:
            made.wait_recv()


class GatherNear:
    def __init__(self, net, part):
        self.net, self.part = net, part

    def start(self):
        n = self.net
        own = self.part(n.y * 2 + n.c, None)
        self.near = [n.copy(own, own, n.at(y=(n.y + o) % NY)) for o in (1, 3, 2)]
        self.over = [n.copy(own, own, n.at(c=1 - n.c))]

    def relay(self):
        n = self.net
        for o, made in zip((1, 3, 2), self.near):
            made.wait_recv()
            slot = self.part((n.y + NY - o) % NY * 2 + n.c, None)
            self.over.append(n.copy(slot, slot, n.at(c=1 - n.c)))

    def done(self):
        for made in self.over:
            made.wait_recv()


class GatherMp:
    def __init__(self, net, block):
        self.net, self.block = net, block

    def start(self):
        n = self.net
        own = self.block.at[n.z, n.x]
        self.a = [n.copy(own, own, n.at(x=(n.x + o) % NX)) for o in range(1, NX)]
        self.s = 0

    def step(self):
        n, s = self.net, self.s
        if s == 0:
            for made in self.a:
                made.wait_recv()
        else:
            self.up.wait_recv()
            self.down.wait_recv()
        if s < NZ // 2:
            up, down = (n.z + NZ - s) % NZ, (n.z + s) % NZ
            if s < NZ // 2 - 1:
                up, down = self.block.at[up], self.block.at[down]
            else:
                half = NX // 2
                up, down = self.block.at[up, pl.ds(0, half)], self.block.at[down, pl.ds(half, half)]
            self.up = n.copy(up, up, n.at(z=(n.z + 1) % NZ))
            self.down = n.copy(down, down, n.at(z=(n.z + NZ - 1) % NZ))
        self.s += 1


def body(x_hbm, g_hbm, w_hbm, ei_hbm, di_hbm, eo_hbm, do_hbm, post_ref, gin_ref,
         xin, g, w, ei, di, eo, do, part, got_x, row, got_z, full, edits, grads, total, cot,
         bpart, bgot_x, brow, bgot_z, zpart, zgot_z, zrow, zgot_x, send, recv, load):
    net = Links(send, recv)
    z, x, y, c = net.z, net.x, net.y, net.c
    d = y * 2 + c

    loads = []
    for k, (src, dst) in enumerate(((x_hbm, xin.at[z, x]), (ei_hbm, ei), (g_hbm, g), (eo_hbm, eo),
                                    (di_hbm, di), (do_hbm, do), (w_hbm, w.at[d]))):
        made = pltpu.make_async_copy(src, dst, load.at[k])
        made.start()
        loads.append(made)

    barrier = pltpu.get_barrier_semaphore()
    peers = ([net.at(x=(x + o) % NX) for o in range(1, NX)] + [net.at(z=(z + o) % NZ) for o in range(1, NZ)]
             + [net.at(y=(y + o) % NY) for o in range(1, NY)] + [net.at(c=1 - c)])
    for peer in peers:
        pl.semaphore_signal(barrier, inc=1, device_id=peer, device_id_type=MESH)

    def w_part(slot, half):
        return w.at[slot] if half is None else w.at[slot, pl.ds(2 * half, 2)]

    def rows_of(ref):
        def pick(slot, half):
            count = TOK if half is None else TOK // 2
            return ref.at[pl.ds(pl.multiple_of(slot * TOK + (half or 0) * count, 32), count)]
        return pick

    whole_w = GatherDp(net, w_part)
    whole_in = GatherMp(net, xin)
    loads[0].wait()
    own = xin[z, x]

    def project(value, enc, out):
        for k in range(7):
            block = nn(value, enc[:, 256 * k:256 * k + 256])
            out[:, k] = block.astype(BF16).reshape(NX, ROWS, 256)
        last = nn(value, enc[:, 1792:1920])
        out[:, 7, :, 0:128] = last.astype(BF16).reshape(NX, ROWS, 128)
        wide = value.astype(F32)
        square = wide * wide
        fold = square[:, 0:128]
        for k in range(1, value.shape[1] // 128):
            fold = fold + square[:, 128 * k:128 * k + 128]
        out[:, 7, :, 128:256] = fold.astype(BF16).reshape(NX, ROWS, 128)

    reduce_in, reduce_out, reduce_kernel, reduce_back = [
        AllReduce(net, part.at[k], got_x.at[k], row.at[k], got_z.at[k], full.at[k], 8 if k < 2 else 6)
        for k in range(4)]

    loads[1].wait()
    project(own, ei, part.at[0])
    pl.semaphore_wait(barrier, len(peers))
    reduce_in.scatter_x()
    whole_w.start(w_hbm)
    loads[2].wait()
    loads[3].wait()
    project(g[...], eo, part.at[1])
    total[...] = jnp.zeros_like(total)
    for made in loads[4:]:
        made.wait()
    reduce_in.scatter_z()
    reduce_out.scatter_x()
    whole_in.start()
    reduce_in.gather_z()
    reduce_in.gather_x()
    whole_in.step()
    reduce_out.scatter_z()

    def edit(value, hidden, dec, features):
        squares = hidden[:, 7, :, 128:256].astype(F32).reshape(TOK, 128)
        scale = lax.rsqrt(jnp.sum(squares, axis=1, keepdims=True) / features + epsilon)
        out = value.astype(F32)
        for k in range(8):
            width = 256 if k < 7 else 128
            h = hidden[:, k, :, 0:width].astype(F32).reshape(TOK, width)
            h = jnp.maximum(h * scale, 0.0).astype(BF16)
            out = out + nn(h, dec[256 * k:256 * k + width, :])
        return out.astype(BF16)

    gather_edits = GatherNear(net, rows_of(edits))
    gather_grads = GatherNear(net, rows_of(grads))
    reduce_in.done()
    rows_own = pl.ds(pl.multiple_of(d * TOK, 64), TOK)
    edits[rows_own, :] = edit(own, full.at[0], di, D)
    gather_edits.start()
    reduce_out.gather_z()
    gather_edits.relay()
    whole_in.step()
    gather_edits.done()

    def inner(k, _):
        some = edits[pl.ds(pl.multiple_of(k * 256, 256), 256), :]
        part[2, :, k] = nt(own, some).astype(BF16).reshape(NX, ROWS, 256)
        return 0
    lax.fori_loop(0, 6, inner, 0)
    reduce_kernel.scatter_x()
    whole_w.relay()
    reduce_kernel.scatter_z()
    reduce_out.gather_x()
    whole_in.step()
    reduce_kernel.gather_z()
    reduce_out.done()
    grads[rows_own, :] = edit(g[...], full.at[1], do, FW)
    gather_grads.start()
    whole_in.step()
    whole_w.relay_far()
    reduce_kernel.gather_x()
    gather_grads.relay()
    whole_in.step()
    whole_w.done()

    def base(k, _):
        value = nn(xin[k, 0], w[k, 0])
        for j in range(1, NX):
            value = value + nn(xin[k, j], w[k, j])
        total[...] += value
        return 0
    lax.fori_loop(0, NZ, base, 0)
    gather_grads.done()
    reduce_kernel.done()

    def correct(k, _):
        block = (full[2, :, k].astype(F32) * FACTOR).astype(BF16).reshape(TOK, 256)
        total[...] -= nn(block, grads[pl.ds(pl.multiple_of(k * 256, 256), 256), :])
        return 0
    lax.fori_loop(0, 6, correct, 0)

    def activate(k, _):
        rows = pl.ds(k * ROWS, ROWS)
        post = total[rows, :]
        post_ref[rows, :] = post.astype(BF16)
        sig = jax.nn.sigmoid(post)
        cot[rows, :] = (g[rows, :].astype(F32) * (sig * (1.0 + post * (1.0 - sig)))).astype(BF16)
        return 0
    lax.fori_loop(0, NX, activate, 0)

    def back_inner(k, _):
        some = grads[pl.ds(pl.multiple_of(k * 256, 256), 256), :]
        part[3, :, k] = nt(cot[...], some).astype(BF16).reshape(NX, ROWS, 256)
        return 0
    lax.fori_loop(0, 6, back_inner, 0)
    reduce_back.scatter_x()

    def back_block(k, _):
        for j in range(NX):
            value = nt(cot[...], w[k, j]).astype(BF16).reshape(NX, ROWS, 256)
            for p in range(3):
                bpart[p, j, k] = value[p]
            zpart[k, j] = value[3]
        return 0
    lax.fori_loop(0, NZ, back_block, 0)
    pieces = [RelayedScatter(net, bpart.at[p], bgot_x.at[p], brow.at[p], bgot_z.at[p], None) for p in range(3)]
    last = ScatterZX(net, zpart, zgot_z, zrow, zgot_x)
    pieces[0].scatter_x()
    last.scatter_z()
    pieces[1].scatter_x()
    reduce_back.scatter_z()
    pieces[0].relay_x()
    pieces[2].scatter_x()
    pieces[1].relay_x()
    pieces[0].scatter_z()
    pieces[2].relay_x()
    reduce_back.gather_z()
    pieces[1].scatter_z()
    last.scatter_x()
    pieces[2].scatter_z()
    reduce_back.gather_x()
    reduce_back.done()
    result = jnp.zeros((TOK, 256), F32)
    for k in range(6):
        block = (full[3, :, k].astype(F32) * FACTOR).astype(BF16).reshape(TOK, 256)
        result = result - nn(block, edits[256 * k:256 * k + 256, :])
    sums = [last.sum_x()]
    sums = [piece.sum_z() for piece in pieces] + sums
    for p in range(NX):
        rows = slice(ROWS * p, ROWS * p + ROWS)
        gin_ref[rows, :] = (result[rows] + sums[p]).astype(BF16)

    net.finish()


COPIES = 176


def shards(inputs, out_grads, weight, enc_in, dec_in, enc_out, dec_out):
    anywhere = pl.BlockSpec(memory_space=pl.ANY)
    vmem = pl.BlockSpec(memory_space=pltpu.VMEM)
    scratch = [
        pltpu.VMEM((NZ, NX, TOK, 256), BF16),
        pltpu.VMEM((TOK, 512), BF16),
        pltpu.VMEM((8, 4, 256, 512), BF16),
        pltpu.VMEM((256, R), BF16),
        pltpu.VMEM((R, 256), BF16),
        pltpu.VMEM((512, R), BF16),
        pltpu.VMEM((R, 512), BF16),
        pltpu.VMEM((4, NX, NZ, ROWS, 256), BF16),
        pltpu.VMEM((4, NX - 1, NZ, ROWS, 256), BF16),
        pltpu.VMEM((4, NZ, ROWS, 256), BF16),
        pltpu.VMEM((4, NZ - 1, ROWS, 256), BF16),
        pltpu.VMEM((4, NX, NZ, ROWS, 256), BF16),
        pltpu.VMEM((8 * TOK, 256), BF16),
        pltpu.VMEM((8 * TOK, 512), BF16),
        pltpu.VMEM((TOK, 512), F32),
        pltpu.VMEM((TOK, 512), BF16),
        pltpu.VMEM((3, NX, NZ, ROWS, 256), BF16),
        pltpu.VMEM((3, NX - 1, NZ, ROWS, 256), BF16),
        pltpu.VMEM((3, NZ, ROWS, 256), BF16),
        pltpu.VMEM((3, NZ - 1, ROWS, 256), BF16),
        pltpu.VMEM((NZ, NX, ROWS, 256), BF16),
        pltpu.VMEM((NZ - 1, NX, ROWS, 256), BF16),
        pltpu.VMEM((NX, ROWS, 256), BF16),
        pltpu.VMEM((NX - 1, ROWS, 256), BF16),
        pltpu.SemaphoreType.DMA((COPIES,)),
        pltpu.SemaphoreType.DMA((COPIES,)),
        pltpu.SemaphoreType.DMA((7,)),
    ]
    return pl.pallas_call(
        body,
        out_shape=(jax.ShapeDtypeStruct((TOK, 512), BF16), jax.ShapeDtypeStruct((TOK, 256), BF16)),
        in_specs=[anywhere] * 7,
        out_specs=(vmem, vmem),
        scratch_shapes=scratch,
        compiler_params=pltpu.CompilerParams(
            collective_id=0, has_side_effects=True, vmem_limit_bytes=60 * 1024 * 1024),
    )(inputs, out_grads, weight.reshape(4, 256, 512), enc_in, dec_in, enc_out, dec_out)


def solution(mesh):
    in_specs = (
        P("dp", "mp"),
        P("dp", "mp"),
        P("dp", "mp"),
        P("mp", None),
        P(None, "mp"),
        P("mp", None),
        P(None, "mp"),
    )
    out_specs = (P("dp", "mp"), P("dp", "mp"))
    return jax.shard_map(shards, mesh=mesh, in_specs=in_specs, out_specs=out_specs, check_vma=False)
```

```python
import functools

import jax
import jax.numpy as jnp
from jax import lax
from jax.experimental import pallas as pl
from jax.experimental.pallas import tpu as pltpu
from jax.sharding import PartitionSpec as P

D = 8192
FW = 16384
R = 1920
NZ, NX, NY = 8, 4, 4
TOK = 192
ROWS = TOK // NX
epsilon = 1e-06
FACTOR = 0.25 / D
F32 = jnp.float32
BF16 = jnp.bfloat16
MESH = pl.DeviceIdType.MESH


def nn(a, b):
    return lax.dot_general(a, b, (((1,), (0,)), ((), ())), preferred_element_type=F32)


def nt(a, b):
    return lax.dot_general(a, b, (((1,), (1,)), ((), ())), preferred_element_type=F32)


def given(when, act):
    if when is None:
        act()
    else:
        pl.when(when)(act)


class Links:
    def __init__(self, send, recv):
        self.send, self.recv, self.used, self.sent = send, recv, 0, []
        mp, dp = lax.axis_index("mp"), lax.axis_index("dp")
        self.z, self.x = mp // NX, mp % NX
        self.y, self.c = dp // 2, dp % 2

    def at(self, z=None, x=None, y=None, c=None):
        z = self.z if z is None else z
        x = self.x if x is None else x
        y = self.y if y is None else y
        c = self.c if c is None else c
        return (z * NX + x, y * 2 + c)

    def copy(self, src, dst, device, when=None):
        k = self.used
        self.used += 1
        made = pltpu.make_async_remote_copy(
            src_ref=src, dst_ref=dst, send_sem=self.send.at[k], recv_sem=self.recv.at[k],
            device_id=device, device_id_type=MESH)
        given(when, made.start)
        self.sent.append((made, when))
        return made

    def finish(self):
        for made, when in self.sent:
            given(when, made.wait_send)


class AllReduce:
    arrivals = NX - 1

    def __init__(self, net, part, got_x, row, got_z, full, blocks=NZ):
        self.net, self.part, self.got_x, self.row, self.got_z, self.full = net, part, got_x, row, got_z, full
        self.blocks = blocks

    def all(self, ref, i):
        return ref.at[i] if self.blocks == NZ else ref.at[i, pl.ds(0, self.blocks)]

    def keeps(self, z):
        return None if self.blocks == NZ else z % 4 != 3

    def block(self, z):
        return z if self.blocks == NZ else z // 4 * 3 + jnp.minimum(z % 4, 2)

    def scatter_x(self):
        n = self.net
        self.a = [n.copy(self.all(self.part, (n.x + o) % NX), self.all(self.got_x, o - 1), n.at(x=(n.x + o) % NX))
                  for o in range(1, NX)]

    def scatter_z(self):
        n = self.net
        for made in self.a:
            made.wait_recv()

        def add(k, _):
            total = self.part[n.x, k].astype(F32)
            for o in range(self.arrivals):
                total = total + self.got_x[o, k].astype(F32)
            self.row[k] = total.astype(BF16)
            return 0
        lax.fori_loop(0, self.blocks, add, 0)
        self.b = []
        for o in range(1, NZ):
            to = (n.z + o) % NZ
            self.b.append(n.copy(self.row.at[self.block(to)], self.got_z.at[o - 1], n.at(z=to), self.keeps(to)))

    def sum_z(self):
        for made in self.b:
            made.wait_recv()
        total = self.row[self.block(self.net.z)].astype(F32)
        for o in range(NZ - 1):
            total = total + self.got_z[o].astype(F32)
        return total

    def gather_z(self):
        n = self.net
        mine = self.block(n.z)

        def settle():
            self.full[n.x, mine] = self.sum_z().astype(BF16)
        given(self.keeps(n.z), settle)
        self.d = [n.copy(self.full.at[n.x, mine], self.full.at[n.x, mine], n.at(z=(n.z + o) % NZ), self.keeps(n.z))
                  for o in range(1, NZ)]

    def gather_x(self):
        n = self.net
        for o, made in enumerate(self.d, 1):
            given(self.keeps((n.z + NZ - o) % NZ), made.wait_recv)
        own = self.all(self.full, n.x)
        self.e = [n.copy(own, own, n.at(x=(n.x + o) % NX)) for o in range(1, NX)]

    def done(self):
        for made in self.e:
            made.wait_recv()


class RelayedScatter(AllReduce):
    arrivals = 2

    def scatter_x(self):
        n, half = self.net, NZ // 2
        far = (n.x + 2) % NX
        low, high = pl.ds(0, half), pl.ds(half, half)
        self.far_up = n.copy(self.part.at[far, low], self.got_x.at[2, low], n.at(x=(n.x + 1) % NX))
        self.far_down = n.copy(self.part.at[far, high], self.got_x.at[2, high], n.at(x=(n.x + 3) % NX))

    def relay_x(self):
        n, half = self.net, NZ // 2
        up, down = (n.x + 1) % NX, (n.x + 3) % NX
        self.far_up.wait_recv()
        self.far_down.wait_recv()

        def add(k, _):
            self.part[up, k] = (self.part[up, k].astype(F32) + self.got_x[2, k].astype(F32)).astype(BF16)
            h = k + half
            self.part[down, h] = (self.part[down, h].astype(F32) + self.got_x[2, h].astype(F32)).astype(BF16)
            return 0
        lax.fori_loop(0, half, add, 0)
        self.a = [n.copy(self.part.at[up], self.got_x.at[0], n.at(x=up)),
                  n.copy(self.part.at[down], self.got_x.at[1], n.at(x=down))]


class ScatterZX:
    def __init__(self, net, part, got_z, row, got_x):
        self.net, self.part, self.got_z, self.row, self.got_x = net, part, got_z, row, got_x

    def scatter_z(self):
        n = self.net
        self.a = [n.copy(self.part.at[(n.z + o) % NZ], self.got_z.at[o - 1], n.at(z=(n.z + o) % NZ))
                  for o in range(1, NZ)]

    def scatter_x(self):
        n = self.net
        for made in self.a:
            made.wait_recv()

        def add(k, _):
            total = self.part[n.z, k].astype(F32)
            for o in range(NZ - 1):
                total = total + self.got_z[o, k].astype(F32)
            self.row[k] = total.astype(BF16)
            return 0
        lax.fori_loop(0, NX, add, 0)
        self.b = [n.copy(self.row.at[(n.x + o) % NX], self.got_x.at[o - 1], n.at(x=(n.x + o) % NX))
                  for o in range(1, NX)]

    def sum_x(self):
        for made in self.b:
            made.wait_recv()
        total = self.row[self.net.x].astype(F32)
        for o in range(NX - 1):
            total = total + self.got_x[o].astype(F32)
        return total


class GatherDp:
    def __init__(self, net, part):
        self.net, self.part = net, part

    def start(self, src=None):
        n = self.net
        d = n.y * 2 + n.c
        own = self.part(d, None)
        src = own if src is None else src
        self.up = n.copy(src, own, n.at(y=(n.y + 1) % NY))
        self.down = n.copy(src, own, n.at(y=(n.y + NY - 1) % NY))
        self.over = [n.copy(src, own, n.at(c=1 - n.c))]

    def relay(self):
        n = self.net
        below = ((n.y + NY - 1) % NY) * 2 + n.c
        above = ((n.y + 1) % NY) * 2 + n.c
        self.up.wait_recv()
        self.up2 = n.copy(self.part(below, 0), self.part(below, 0), n.at(y=(n.y + 1) % NY))
        self.over.append(n.copy(self.part(below, None), self.part(below, None), n.at(c=1 - n.c)))
        self.down.wait_recv()
        self.down2 = n.copy(self.part(above, 1), self.part(above, 1), n.at(y=(n.y + NY - 1) % NY))
        self.over.append(n.copy(self.part(above, None), self.part(above, None), n.at(c=1 - n.c)))

    def relay_far(self):
        n = self.net
        far = ((n.y + 2) % NY) * 2 + n.c
        self.up2.wait_recv()
        self.over.append(n.copy(self.part(far, 0), self.part(far, 0), n.at(c=1 - n.c)))
        self.down2.wait_recv()
        self.over.append(n.copy(self.part(far, 1), self.part(far, 1), n.at(c=1 - n.c)))

    def done(self):
        for made in self.over:
            made.wait_recv()


class GatherNear:
    def __init__(self, net, part):
        self.net, self.part = net, part

    def start(self):
        n = self.net
        own = self.part(n.y * 2 + n.c, None)
        self.near = [n.copy(own, own, n.at(y=(n.y + o) % NY)) for o in (1, 3, 2)]
        self.over = [n.copy(own, own, n.at(c=1 - n.c))]

    def relay(self):
        n = self.net
        for o, made in zip((1, 3, 2), self.near):
            made.wait_recv()
            slot = self.part((n.y + NY - o) % NY * 2 + n.c, None)
            self.over.append(n.copy(slot, slot, n.at(c=1 - n.c)))

    def done(self):
        for made in self.over:
            made.wait_recv()


class GatherMp:
    def __init__(self, net, block):
        self.net, self.block = net, block

    def start(self):
        n = self.net
        own = self.block.at[n.z, n.x]
        self.a = [n.copy(own, own, n.at(x=(n.x + o) % NX)) for o in range(1, NX)]
        self.s = 0

    def step(self):
        n, s = self.net, self.s
        if s == 0:
            for made in self.a:
                made.wait_recv()
        else:
            self.up.wait_recv()
            self.down.wait_recv()
        if s < NZ // 2:
            up, down = (n.z + NZ - s) % NZ, (n.z + s) % NZ
            if s < NZ // 2 - 1:
                up, down = self.block.at[up], self.block.at[down]
            else:
                half = NX // 2
                up, down = self.block.at[up, pl.ds(0, half)], self.block.at[down, pl.ds(half, half)]
            self.up = n.copy(up, up, n.at(z=(n.z + 1) % NZ))
            self.down = n.copy(down, down, n.at(z=(n.z + NZ - 1) % NZ))
        self.s += 1


def body(x_hbm, g_hbm, w_hbm, ei_hbm, di_hbm, eo_hbm, do_hbm, post_ref, gin_ref,
         xin, g, w, ei, di, eo, do, part, got_x, row, got_z, full, edits, grads, total, cot,
         bpart, bgot_x, brow, bgot_z, zpart, zgot_z, zrow, zgot_x, send, recv, load):
    net = Links(send, recv)
    z, x, y, c = net.z, net.x, net.y, net.c
    d = y * 2 + c

    loads = []
    for k, (src, dst) in enumerate(((x_hbm, xin.at[z, x]), (ei_hbm, ei), (g_hbm, g), (eo_hbm, eo),
                                    (di_hbm, di), (do_hbm, do), (w_hbm, w.at[d]))):
        made = pltpu.make_async_copy(src, dst, load.at[k])
        made.start()
        loads.append(made)

    barrier = pltpu.get_barrier_semaphore()
    peers = ([net.at(x=(x + o) % NX) for o in range(1, NX)] + [net.at(z=(z + o) % NZ) for o in range(1, NZ)]
             + [net.at(y=(y + o) % NY) for o in range(1, NY)] + [net.at(c=1 - c)])
    for peer in peers:
        pl.semaphore_signal(barrier, inc=1, device_id=peer, device_id_type=MESH)

    def w_part(slot, half):
        return w.at[slot] if half is None else w.at[slot, pl.ds(2 * half, 2)]

    def rows_of(ref):
        def pick(slot, half):
            count = TOK if half is None else TOK // 2
            return ref.at[pl.ds(pl.multiple_of(slot * TOK + (half or 0) * count, 32), count)]
        return pick

    whole_w = GatherDp(net, w_part)
    whole_in = GatherMp(net, xin)
    loads[0].wait()
    own = xin[z, x]

    def project(value, enc, out):
        for k in range(7):
            block = nn(value, enc[:, 256 * k:256 * k + 256])
            out[:, k] = block.astype(BF16).reshape(NX, ROWS, 256)
        last = nn(value, enc[:, 1792:1920])
        out[:, 7, :, 0:128] = last.astype(BF16).reshape(NX, ROWS, 128)
        wide = value.astype(F32)
        square = wide * wide
        fold = square[:, 0:128]
        for k in range(1, value.shape[1] // 128):
            fold = fold + square[:, 128 * k:128 * k + 128]
        out[:, 7, :, 128:256] = fold.astype(BF16).reshape(NX, ROWS, 128)

    reduce_in, reduce_out, reduce_kernel, reduce_back = [
        AllReduce(net, part.at[k], got_x.at[k], row.at[k], got_z.at[k], full.at[k], 8 if k < 2 else 6)
        for k in range(4)]

    loads[1].wait()
    project(own, ei, part.at[0])
    pl.semaphore_wait(barrier, len(peers))
    reduce_in.scatter_x()
    whole_w.start(w_hbm)
    loads[2].wait()
    loads[3].wait()
    project(g[...], eo, part.at[1])
    total[...] = jnp.zeros_like(total)
    for made in loads[4:]:
        made.wait()
    reduce_in.scatter_z()
    reduce_out.scatter_x()
    whole_in.start()
    reduce_in.gather_z()
    reduce_in.gather_x()
    whole_in.step()
    reduce_out.scatter_z()

    def edit(value, hidden, dec, features):
        squares = hidden[:, 7, :, 128:256].astype(F32).reshape(TOK, 128)
        scale = lax.rsqrt(jnp.sum(squares, axis=1, keepdims=True) / features + epsilon)
        out = value.astype(F32)
        for k in range(8):
            width = 256 if k < 7 else 128
            h = hidden[:, k, :, 0:width].astype(F32).reshape(TOK, width)
            h = jnp.maximum(h * scale, 0.0).astype(BF16)
            out = out + nn(h, dec[256 * k:256 * k + width, :])
        return out.astype(BF16)

    gather_edits = GatherNear(net, rows_of(edits))
    gather_grads = GatherNear(net, rows_of(grads))
    reduce_in.done()
    rows_own = pl.ds(pl.multiple_of(d * TOK, 64), TOK)
    edits[rows_own, :] = edit(own, full.at[0], di, D)
    gather_edits.start()
    reduce_out.gather_z()
    gather_edits.relay()
    whole_in.step()
    gather_edits.done()

    def inner(k, _):
        some = edits[pl.ds(pl.multiple_of(k * 256, 256), 256), :]
        part[2, :, k] = nt(own, some).astype(BF16).reshape(NX, ROWS, 256)
        return 0
    lax.fori_loop(0, 6, inner, 0)
    reduce_kernel.scatter_x()
    whole_w.relay()
    reduce_kernel.scatter_z()
    reduce_out.gather_x()
    whole_in.step()
    reduce_kernel.gather_z()
    reduce_out.done()
    grads[rows_own, :] = edit(g[...], full.at[1], do, FW)
    gather_grads.start()
    whole_in.step()
    whole_w.relay_far()
    reduce_kernel.gather_x()
    gather_grads.relay()
    whole_in.step()
    whole_w.done()

    def base(k, _):
        value = nn(xin[k, 0], w[k, 0])
        for j in range(1, NX):
            value = value + nn(xin[k, j], w[k, j])
        total[...] += value
        return 0
    lax.fori_loop(0, NZ, base, 0)
    gather_grads.done()
    reduce_kernel.done()

    def correct(k, _):
        block = (full[2, :, k].astype(F32) * FACTOR).astype(BF16).reshape(TOK, 256)
        total[...] -= nn(block, grads[pl.ds(pl.multiple_of(k * 256, 256), 256), :])
        return 0
    lax.fori_loop(0, 6, correct, 0)

    def activate(k, _):
        rows = pl.ds(k * ROWS, ROWS)
        post = total[rows, :]
        post_ref[rows, :] = post.astype(BF16)
        sig = jax.nn.sigmoid(post)
        cot[rows, :] = (g[rows, :].astype(F32) * (sig * (1.0 + post * (1.0 - sig)))).astype(BF16)
        return 0
    lax.fori_loop(0, NX, activate, 0)

    def back_inner(k, _):
        some = grads[pl.ds(pl.multiple_of(k * 256, 256), 256), :]
        part[3, :, k] = nt(cot[...], some).astype(BF16).reshape(NX, ROWS, 256)
        return 0
    lax.fori_loop(0, 6, back_inner, 0)
    reduce_back.scatter_x()

    def back_block(k, _):
        for j in range(NX):
            value = nt(cot[...], w[k, j]).astype(BF16).reshape(NX, ROWS, 256)
            for p in range(3):
                bpart[p, j, k] = value[p]
            zpart[k, j] = value[3]
        return 0
    lax.fori_loop(0, NZ, back_block, 0)
    pieces = [RelayedScatter(net, bpart.at[p], bgot_x.at[p], brow.at[p], bgot_z.at[p], None) for p in range(3)]
    last = ScatterZX(net, zpart, zgot_z, zrow, zgot_x)
    pieces[0].scatter_x()
    last.scatter_z()
    pieces[1].scatter_x()
    reduce_back.scatter_z()
    pieces[0].relay_x()
    pieces[2].scatter_x()
    pieces[1].relay_x()
    pieces[0].scatter_z()
    pieces[2].relay_x()
    reduce_back.gather_z()
    pieces[1].scatter_z()
    reduce_back.gather_x()
    pieces[2].scatter_z()
    last.scatter_x()
    reduce_back.done()
    result = jnp.zeros((TOK, 256), F32)
    for k in range(6):
        block = (full[3, :, k].astype(F32) * FACTOR).astype(BF16).reshape(TOK, 256)
        result = result - nn(block, edits[256 * k:256 * k + 256, :])
    sums = [last.sum_x()]
    sums = [piece.sum_z() for piece in pieces] + sums
    for p in range(NX):
        rows = slice(ROWS * p, ROWS * p + ROWS)
        gin_ref[rows, :] = (result[rows] + sums[p]).astype(BF16)

    net.finish()


COPIES = 176


def shards(inputs, out_grads, weight, enc_in, dec_in, enc_out, dec_out):
    anywhere = pl.BlockSpec(memory_space=pl.ANY)
    vmem = pl.BlockSpec(memory_space=pltpu.VMEM)
    scratch = [
        pltpu.VMEM((NZ, NX, TOK, 256), BF16),
        pltpu.VMEM((TOK, 512), BF16),
        pltpu.VMEM((8, 4, 256, 512), BF16),
        pltpu.VMEM((256, R), BF16),
        pltpu.VMEM((R, 256), BF16),
        pltpu.VMEM((512, R), BF16),
        pltpu.VMEM((R, 512), BF16),
        pltpu.VMEM((4, NX, NZ, ROWS, 256), BF16),
        pltpu.VMEM((4, NX - 1, NZ, ROWS, 256), BF16),
        pltpu.VMEM((4, NZ, ROWS, 256), BF16),
        pltpu.VMEM((4, NZ - 1, ROWS, 256), BF16),
        pltpu.VMEM((4, NX, NZ, ROWS, 256), BF16),
        pltpu.VMEM((8 * TOK, 256), BF16),
        pltpu.VMEM((8 * TOK, 512), BF16),
        pltpu.VMEM((TOK, 512), F32),
        pltpu.VMEM((TOK, 512), BF16),
        pltpu.VMEM((3, NX, NZ, ROWS, 256), BF16),
        pltpu.VMEM((3, NX - 1, NZ, ROWS, 256), BF16),
        pltpu.VMEM((3, NZ, ROWS, 256), BF16),
        pltpu.VMEM((3, NZ - 1, ROWS, 256), BF16),
        pltpu.VMEM((NZ, NX, ROWS, 256), BF16),
        pltpu.VMEM((NZ - 1, NX, ROWS, 256), BF16),
        pltpu.VMEM((NX, ROWS, 256), BF16),
        pltpu.VMEM((NX - 1, ROWS, 256), BF16),
        pltpu.SemaphoreType.DMA((COPIES,)),
        pltpu.SemaphoreType.DMA((COPIES,)),
        pltpu.SemaphoreType.DMA((7,)),
    ]
    return pl.pallas_call(
        body,
        out_shape=(jax.ShapeDtypeStruct((TOK, 512), BF16), jax.ShapeDtypeStruct((TOK, 256), BF16)),
        in_specs=[anywhere] * 7,
        out_specs=(vmem, vmem),
        scratch_shapes=scratch,
        compiler_params=pltpu.CompilerParams(
            collective_id=0, has_side_effects=True, vmem_limit_bytes=60 * 1024 * 1024),
    )(inputs, out_grads, weight.reshape(4, 256, 512), enc_in, dec_in, enc_out, dec_out)


def solution(mesh):
    in_specs = (
        P("dp", "mp"),
        P("dp", "mp"),
        P("dp", "mp"),
        P("mp", None),
        P(None, "mp"),
        P("mp", None),
        P(None, "mp"),
    )
    out_specs = (P("dp", "mp"), P("dp", "mp"))
    return jax.shard_map(shards, mesh=mesh, in_specs=in_specs, out_specs=out_specs, check_vma=False)
```
